32 devices in a mesh: depth: 16 (over z, y, core), cols: 2 (over x).
Axes of the slice: x: 2, y: 2, z: 4, core: 2. Of those that a mesh axis runs over, the one named last changes fastest.
Arguments:
- field: float32 [32, 2048, 256], P('depth', None, 'cols'), may hold values from -6 to 6
Outputs:
- picture: float32 [4, 2048, 256], P(None, 'depth', 'cols')
The draws below stay inside these ranges and needn't reach their ends.
All inputs are finite; a program needn't handle non-finite values.
Results may differ from the reference program's by a relative error of at most 0.00002.
Values sent between devices are 32-bit elements; how exact they have to be, the bound alone decides.
No kernel may reach another device: no remote copies, remote signals or barrier semaphores. Data moves between devices by JAX's collectives and lax.ppermute only.
A program may use at most 128 MiB of HBM per device.

```python
import math
import jax
import jax.numpy as jnp
from jax import lax

ROWS = 2048
NZ = 32
WIDTH = 256


def block_levels(stream_key, dims, cuts, low, high):
    gain, own = 1.0, jax.random.fold_in(stream_key, 6)
    for dim, shards_of in cuts:
        heights = jnp.exp(jax.random.uniform(jax.random.fold_in(own, dim), (shards_of,), jnp.float32, low / len(cuts), high / len(cuts)))
        gain = gain * jnp.repeat(heights, dims[dim] // shards_of).reshape([-1 if axis == dim else 1 for axis in range(len(dims))])
    return gain


def noise(own_key, dims, spread, reach, cuts=(), dtype=jnp.bfloat16):
    entries = spread * jax.random.normal(own_key, dims, jnp.float32)
    if cuts:
        entries = entries * block_levels(own_key, dims, cuts, -0.22, 0.18)
    return jnp.clip(entries, -reach, reach).astype(dtype)


def setup_inputs(seed: int = 0) -> dict:
    key_of = jax.random.split(jax.random.key(seed), 2)
    field = noise(key_of[0], (NZ, ROWS, WIDTH), 1.0, 6.0, ((0, 16), (2, 2)), jnp.float32)
    return {"field": field}


def apply_taps(array_in, tap_list, which_axis):
    length = array_in.shape[which_axis] - 4
    result = tap_list[0] * lax.slice_in_dim(array_in, 0, length, axis=which_axis)
    for offset in range(1, 5):
        result = result + tap_list[offset] * lax.slice_in_dim(array_in, offset, offset + length, axis=which_axis)
    return result

def render_slab(padded):
    gauss_taps = [1.0 / 16, 4.0 / 16, 6.0 / 16, 4.0 / 16, 1.0 / 16]
    deriv_taps = [-1.0 / 8, -2.0 / 8, 0.0, 2.0 / 8, 1.0 / 8]
    smooth_x = apply_taps(padded, gauss_taps, 2)
    deriv_x = apply_taps(padded, deriv_taps, 2)
    smooth_xy = apply_taps(smooth_x, gauss_taps, 1)
    deriv_y = apply_taps(smooth_x, deriv_taps, 1)
    deriv_xy = apply_taps(deriv_x, gauss_taps, 1)
    smooth = apply_taps(smooth_xy, gauss_taps, 0)
    grad_z = 8.0 * apply_taps(smooth_xy, deriv_taps, 0)
    grad_y = 8.0 * apply_taps(deriv_y, gauss_taps, 0)
    grad_x = 8.0 * apply_taps(deriv_xy, gauss_taps, 0)
    scaled = 7.0 * smooth
    opacity = 0.6 * jax.nn.sigmoid(6.0 * scaled - 13.2)
    norm_len = jnp.sqrt(grad_x * grad_x + grad_y * grad_y + grad_z * grad_z + 1.0)
    half_len = math.sqrt(0.48 * 0.48 + 0.6 * 0.6 + 1.64 * 1.64)
    dot_light = (0.48 * grad_x + 0.6 * grad_y + 0.64 * grad_z) / norm_len
    dot_half = (0.48 * grad_x + 0.6 * grad_y + 1.64 * grad_z) / (half_len * norm_len)
    shading = 0.25 + 0.6 * jnp.maximum(dot_light, 0.0) + 0.35 * jnp.maximum(dot_half, 0.0) ** 8
    weight = opacity * shading
    colours = jnp.stack([jax.nn.sigmoid(2.0 * scaled + 0.5) * weight, (0.5 + 0.4 * jnp.tanh(scaled)) * weight, jax.nn.sigmoid(-2.0 * scaled) * weight], 0)
    return (colours, opacity)

def composite_planes(colours, opacity):

    def step_fn(state_pair, plane):
        colour_sum, opacity_sum = state_pair
        plane_colour, plane_opacity = plane
        remain = 1.0 - opacity_sum
        return ((colour_sum + remain[None] * plane_colour, opacity_sum + remain * plane_opacity), None)
    start = (jnp.zeros(colours.shape[0:1] + colours.shape[2:], jnp.float32), jnp.zeros(opacity.shape[1:], jnp.float32))
    final_pair, unused = lax.scan(step_fn, start, (jnp.moveaxis(colours, 1, 0), opacity))
    return jnp.concatenate([final_pair[0], final_pair[1][None]], 0)

def reference(field):
    padded = jnp.pad(field, 2)
    colours, opacity = render_slab(padded)
    return composite_planes(colours, opacity)
```

```python
import functools
import math

import jax
import jax.numpy as jnp
import numpy as np
from jax import lax
from jax.experimental import pallas as pl
from jax.experimental.pallas import tpu as pltpu
from jax.sharding import PartitionSpec as P

GAUSS = (1.0, 4.0, 6.0, 4.0, 1.0)
DERIV = (-1.0, -2.0, 0.0, 2.0, 1.0)
SCALE = 7.0 / 4096.0
ONE = 49.0 / 256.0
HALF_LEN = math.sqrt(0.48 * 0.48 + 0.6 * 0.6 + 1.64 * 1.64)
SPEC = 0.35 / HALF_LEN**8
LOG2E = 1.0 / math.log(2.0)
LANES = 128
TILE = 16


def column_weights(width):
    body = np.zeros((width, 2 * width), np.float32)
    halo = np.zeros((4, 2 * width), np.float32)
    for out in range(width):
        for k in range(5):
            col = out - 2 + k
            for part, taps in enumerate((GAUSS, DERIV)):
                value = SCALE * taps[k]
                if 0 <= col < width:
                    body[col, part * width + out] = value
                else:
                    halo[col + 2 if col < 0 else col - width + 2, part * width + out] = value
    side = np.zeros((LANES, 2 * width), np.float32)
    for row in range(24):
        side[row] = halo[row % 4]
    return np.concatenate([body, body, body, side], 0).astype(jnp.bfloat16)


def three_parts(x):
    hi = x.astype(jnp.bfloat16)
    rest = x - hi.astype(jnp.float32)
    mid = rest.astype(jnp.bfloat16)
    lo = (rest - mid.astype(jnp.float32)).astype(jnp.bfloat16)
    return hi, mid, lo


def filter_columns(block, plane, rows, weights, sx, dx, slot):
    width = block.shape[2]
    hi, mid, lo = three_parts(block[plane, 0:rows, :])
    sides = [part.astype(jnp.float32) for part in three_parts(block[plane, rows : rows + 8, :])]
    lanes_first = jnp.transpose(jnp.concatenate(sides, 0))
    lane = lax.broadcasted_iota(jnp.int32, lanes_first.shape, 1)
    pieces = []
    for b in range(-(-rows // LANES)):
        mine = jnp.where(lane % 8 // 4 == b, lanes_first, 0.0)
        pieces.append(mine[0 : min(LANES, rows - b * LANES)])
    side = jnp.concatenate(pieces, 0)
    side = jnp.concatenate([side, jnp.zeros((rows, LANES - side.shape[1]), jnp.float32)], 1)
    row = jnp.concatenate([hi, mid, lo, side.astype(jnp.bfloat16)], 1)
    both = jnp.dot(row, weights[...], preferred_element_type=jnp.float32)
    sx[slot] = both[:, :width]
    dx[slot] = both[:, width:]


def gauss_rows(a, b, c, d, e):
    return (a + e) + 4.0 * (b + d) + 6.0 * c


def shade(t, gx, gy, gz, state):
    v_sum, vt_sum, vu_sum, cover = state
    opacity = 0.6 * pl.reciprocal(1.0 + jnp.exp2(jnp.minimum(13.2 * LOG2E - (6.0 * LOG2E) * t, 126.0)))
    tanh_t = jnp.tanh(t)
    tanh_u = jnp.tanh(t + 0.25)
    light = 0.48 * gx + 0.6 * gy + 0.64 * gz
    inv = lax.rsqrt(gx * gx + gy * gy + gz * gz + ONE)
    diffuse = jnp.maximum(light, 0.0) * inv
    half = jnp.maximum(light + gz, 0.0) * inv
    half = half * half
    half = half * half
    shading = 0.25 + 0.6 * diffuse + SPEC * (half * half)
    part = (1.0 - cover) * opacity
    value = part * shading
    return v_sum + value, vt_sum + value * tanh_t, vu_sum + value * tanh_u, cover + part


def render(sx, dx, first, count):
    def rows_of(ref, slot):
        return [ref[slot, pl.ds(first + k, TILE), :] for k in range(5)]

    zero = jnp.zeros((TILE, sx.shape[2]), jnp.float32)
    state = (zero, zero, zero, zero)
    chains = [[None] * 4 for _ in range(3)]
    for index in range(count + 4):
        a, b, c, d, e = rows_of(sx, index)
        inputs = [gauss_rows(a, b, c, d, e), (e - a) + 2.0 * (d - b), gauss_rows(*rows_of(dx, index))]
        totals, diff = [], None
        for which, (chain, x) in enumerate(zip(chains, inputs)):
            for level in range(4):
                before, chain[level] = chain[level], x
                if before is None:
                    x = None
                    break
                if which == 0 and level == 3:
                    diff = x - before
                x = x + before
            totals.append(x)
        if index >= 4:
            state = shade(totals[0], totals[2], totals[1], diff, state)
    return state


def over(front, back):
    rest = 1.0 - front[3]
    return tuple(f + rest * b for f, b in zip(front, back))


def render_kernel(size, last, info, weights, *refs):
    blocks, refs = refs[:size], refs[size:]
    if last:
        boundary, other, image, sx, dx = refs
    else:
        image, sx, dx = refs
    depth, rows = blocks[0].shape[0], sx.shape[1]
    planes = depth * size
    extra = 4 if last else 0
    pos, front = info[0], info[1]
    start = 2 * front + extra * (1 - front)
    empty = (1 - front) * (planes + extra)
    sx[pl.ds(empty, 2)] = jnp.zeros((2,) + sx.shape[1:], jnp.float32)
    dx[pl.ds(empty, 2)] = jnp.zeros((2,) + dx.shape[1:], jnp.float32)
    for step in range(size):
        for plane in range(depth):
            slot = (pos ^ step) * depth + plane + start
            filter_columns(blocks[step], plane, rows, weights, sx, dx, slot)
    for plane in range(extra):
        slot = (planes + 2) * front + plane
        filter_columns(boundary, plane, rows, weights, sx, dx, slot)

    @pl.loop(0, image.shape[1] // TILE)
    def _(tile):
        first = pl.multiple_of(tile * TILE, TILE)
        total = render(sx, dx, first, planes - 2 + extra)
        if last:
            is_front = front == 1
            rest = tuple(other[channel, pl.ds(first, TILE), :] for channel in range(4))
            ahead = tuple(jnp.where(is_front, m, r) for m, r in zip(total, rest))
            behind = tuple(jnp.where(is_front, r, m) for m, r in zip(total, rest))
            v_sum, vt_sum, vu_sum, cover = over(ahead, behind)
            total = (0.5 * (v_sum + vu_sum), 0.5 * v_sum + 0.4 * vt_sum, 0.5 * (v_sum - vt_sum), cover)
        for channel in range(4):
            image[channel, pl.ds(first, TILE), :] = total[channel]


def pack_kernel(size, rows, info, field, sides, *refs):
    outs, padded = refs[:-1], refs[-1]
    depth, height, width = field.shape
    own = rows - 8
    pos, front = info[0], info[1]
    padded[:, 0:8, :] = jnp.zeros((depth, 8, width), jnp.float32)
    padded[:, 8 + height : 16 + height, :] = jnp.zeros((depth, 8, width), jnp.float32)
    padded[:, 8 : 8 + height, :] = field[...]
    for chunk in range(2):
        base = (1 - front) * size if chunk == 0 else front * size
        for step in range(size):
            out = outs[chunk * size + step]
            target = base + (pos ^ step)
            start = pl.multiple_of(target * own, 8)
            for plane in range(depth):
                out[plane, 0:rows, :] = padded[plane, pl.ds(start + 6, rows), :]
                out[plane, rows : rows + 8, :] = sides[target, plane]


def pick_kernel(size, info, *refs):
    blocks, out, sem = refs[:size], refs[size], refs[size + 1]
    depth = blocks[0].shape[0]
    pos, front = info[0], info[1]
    count = 4 // depth
    for part in range(count):
        wanted = pos ^ (front * (size - count) + part)
        for step in range(size):

            @pl.when(wanted == step)
            def _():
                pltpu.make_async_copy(blocks[step], out.at[pl.ds(part * depth, depth)], sem.at[part]).start()

    for part in range(count):
        place = out.at[pl.ds(part * depth, depth)]
        pltpu.make_async_copy(blocks[0], place, sem.at[part]).wait()


SMEM = pl.BlockSpec(memory_space=pltpu.SMEM)
VMEM = pl.BlockSpec(memory_space=pltpu.VMEM)
ANY = pl.BlockSpec(memory_space=pl.ANY)
PARAMS = pltpu.CompilerParams(vmem_limit_bytes=48 * 1024 * 1024)


def cost(flops, size):
    return pl.CostEstimate(flops=flops, bytes_accessed=size, transcendentals=0)


def side_columns(field, own, rows):
    groups = lax.axis_size("cols")
    up = [(i, i + 1) for i in range(groups - 1)]
    down = [(j, i) for i, j in up]
    width = field.shape[2]
    before = lax.ppermute(jnp.transpose(field[:, :, width - 2 :], (2, 0, 1)), "cols", up)
    after = lax.ppermute(jnp.transpose(field[:, :, :2], (2, 0, 1)), "cols", down)
    both = jnp.concatenate([before, after], 0)
    depth, height = both.shape[1:]
    pieces = -(-rows // LANES)
    span = pieces * LANES
    count = height // own
    both = jnp.pad(both, ((0, 0), (0, 0), (2, span)))
    cut = jnp.stack([both[:, :, own * j : own * j + span] for j in range(count)], 0)
    cut = cut.reshape(count, 4, depth, pieces, LANES).transpose(0, 2, 3, 1, 4)
    cut = cut.reshape(count, depth, 4 * pieces, LANES)
    return jnp.pad(cut, ((0, 0), (0, 0), (0, 8 - 4 * pieces), (0, 0)))


def local(field):
    groups = lax.axis_size("depth")
    size = groups // 2
    depth, height, width = field.shape
    own = height // groups
    rows = own + 8
    me = lax.axis_index("depth")
    info = jnp.stack([me % size, 1 - me // size]).astype(jnp.int32)
    weights = jnp.asarray(column_weights(width))
    f32 = jnp.float32
    block = jax.ShapeDtypeStruct((depth, rows + 8, width), f32)
    image = jax.ShapeDtypeStruct((4, own, width), f32)

    sides = side_columns(field, own, rows)
    blocks = pl.pallas_call(
        functools.partial(pack_kernel, size, rows),
        out_shape=(block,) * (2 * size),
        in_specs=[SMEM, VMEM, VMEM],
        out_specs=(VMEM,) * (2 * size),
        scratch_shapes=[pltpu.VMEM((depth, height + 16, width), f32)],
        compiler_params=PARAMS,
        name="pack_blocks",
    )(info, field, sides)

    def render_call(last):
        count = depth * size + (6 if last else 2)
        return pl.pallas_call(
            functools.partial(render_kernel, size, last),
            out_shape=image,
            in_specs=[SMEM] + [VMEM] * (size + (3 if last else 1)),
            out_specs=VMEM,
            scratch_shapes=[pltpu.VMEM((count, rows, width), f32)] * 2,
            compiler_params=PARAMS,
            cost_estimate=cost(5_000_000_000, 2_000_000),
            name="render_last" if last else "render_first",
        )

    pick = pl.pallas_call(
        functools.partial(pick_kernel, size),
        out_shape=jax.ShapeDtypeStruct((4, rows + 8, width), f32),
        in_specs=[SMEM] + [ANY] * size,
        out_specs=ANY,
        scratch_shapes=[pltpu.SemaphoreType.DMA((4 // depth,))],
        name="pick_boundary",
    )

    def swap(x, bits):
        return lax.ppermute(x, "depth", [(i, i ^ bits) for i in range(groups)])

    def gathered(mine):
        return [mine[0]] + [swap(mine[step], step) for step in range(1, size)]

    theirs = gathered(blocks[size:])
    boundary = swap(pick(info, *theirs), size)
    image_part = swap(render_call(False)(info, weights, *theirs), size)
    mine = gathered(blocks[:size])
    return render_call(True)(info, weights, *mine, boundary, image_part)


def solution(mesh):
    return jax.shard_map(
        local,
        mesh=mesh,
        in_specs=(P("depth", None, "cols"),),
        out_specs=P(None, "depth", "cols"),
        check_vma=False,
    )
```

```python
import functools
import math

import jax
import jax.numpy as jnp
import numpy as np
from jax import lax
from jax.experimental import pallas as pl
from jax.experimental.pallas import tpu as pltpu
from jax.sharding import PartitionSpec as P

GAUSS = (1.0, 4.0, 6.0, 4.0, 1.0)
DERIV = (-1.0, -2.0, 0.0, 2.0, 1.0)
SCALE = 7.0 / 4096.0
ONE = 49.0 / 256.0
HALF_LEN = math.sqrt(0.48 * 0.48 + 0.6 * 0.6 + 1.64 * 1.64)
SPEC = 0.35 / HALF_LEN**8
LOG2E = 1.0 / math.log(2.0)
LANES = 128
TILE = 16


def column_weights(width):
    body = np.zeros((width, 2 * width), np.float32)
    halo = np.zeros((4, 2 * width), np.float32)
    for out in range(width):
        for k in range(5):
            col = out - 2 + k
            for part, taps in enumerate((GAUSS, DERIV)):
                value = SCALE * taps[k]
                if 0 <= col < width:
                    body[col, part * width + out] = value
                else:
                    halo[col + 2 if col < 0 else col - width + 2, part * width + out] = value
    side = np.zeros((LANES, 2 * width), np.float32)
    for row in range(24):
        side[row] = halo[row % 4]
    return np.concatenate([body, body, body, side], 0).astype(jnp.bfloat16)


def three_parts(x):
    hi = x.astype(jnp.bfloat16)
    rest = x - hi.astype(jnp.float32)
    mid = rest.astype(jnp.bfloat16)
    lo = (rest - mid.astype(jnp.float32)).astype(jnp.bfloat16)
    return hi, mid, lo


def filter_columns(block, plane, own, weights, sx, dx, slot):
    width = block.shape[-1]
    hi, mid, lo = three_parts(block[plane, 0 : own + 8, :])
    sides = [part.astype(jnp.float32) for part in three_parts(block[plane, own + 8 : own + 16, :])]
    lanes_first = jnp.transpose(jnp.concatenate(sides, 0))
    inner = lax.broadcasted_iota(jnp.int32, lanes_first.shape, 1) % 8 < 4
    side = jnp.concatenate([jnp.where(inner, lanes_first, 0.0)[0:own], jnp.where(inner, 0.0, lanes_first)[0:8]], 0)
    side = jnp.concatenate([side, jnp.zeros((own + 8, LANES - side.shape[1]), jnp.float32)], 1)
    row = jnp.concatenate([hi, mid, lo, side.astype(jnp.bfloat16)], 1)
    both = jnp.dot(row, weights[...], preferred_element_type=jnp.float32)
    for out, part in ((sx, both[:, :width]), (dx, both[:, width:])):
        out[slot, 8 : 8 + own] = part[0:own]
        out[slot, 6:8] = part[own : own + 2]
        out[slot, 8 + own : 10 + own] = part[own + 2 : own + 4]


def gauss_rows(a, b, c, d, e):
    return (a + e) + 4.0 * (b + d) + 6.0 * c


def shade(t, gx, gy, gz, state):
    v_sum, vt_sum, vu_sum, cover = state
    opacity = 0.6 * pl.reciprocal(1.0 + jnp.exp2(jnp.minimum(13.2 * LOG2E - (6.0 * LOG2E) * t, 126.0)))
    tanh_t = jnp.tanh(t)
    tanh_u = jnp.tanh(t + 0.25)
    light = 0.48 * gx + 0.6 * gy + 0.64 * gz
    inv = lax.rsqrt(gx * gx + gy * gy + gz * gz + ONE)
    diffuse = jnp.maximum(light, 0.0) * inv
    half = jnp.maximum(light + gz, 0.0) * inv
    half = half * half
    half = half * half
    shading = 0.25 + 0.6 * diffuse + SPEC * (half * half)
    part = (1.0 - cover) * opacity
    value = part * shading
    return v_sum + value, vt_sum + value * tanh_t, vu_sum + value * tanh_u, cover + part


def render(sx, dx, first, count):
    def rows_of(ref, slot):
        return [ref[slot, pl.ds(first + 6 + k, TILE), :] for k in range(5)]

    zero = jnp.zeros((TILE, sx.shape[2]), jnp.float32)
    state = (zero, zero, zero, zero)
    chains = [[None] * 4 for _ in range(3)]
    for index in range(count + 4):
        a, b, c, d, e = rows_of(sx, index)
        inputs = [gauss_rows(a, b, c, d, e), (e - a) + 2.0 * (d - b), gauss_rows(*rows_of(dx, index))]
        totals, diff = [], None
        for which, (chain, x) in enumerate(zip(chains, inputs)):
            for level in range(4):
                before, chain[level] = chain[level], x
                if before is None:
                    x = None
                    break
                if which == 0 and level == 3:
                    diff = x - before
                x = x + before
            totals.append(x)
        if index >= 4:
            state = shade(totals[0], totals[2], totals[1], diff, state)
    return state


def over(front, back):
    rest = 1.0 - front[3]
    return tuple(f + rest * b for f, b in zip(front, back))


def render_kernel(size, last, info, weights, *refs):
    blocks, refs = refs[:size], refs[size:]
    if last:
        boundary, other, image, sx, dx = refs
    else:
        image, sx, dx = refs
    depth, own = blocks[0].shape[0], image.shape[1]
    planes = depth * size
    extra = 4 if last else 0
    pos, front = info[0], info[1]
    start = 2 * front + extra * (1 - front)
    empty = (1 - front) * (planes + extra)
    sx[pl.ds(empty, 2)] = jnp.zeros((2,) + sx.shape[1:], jnp.float32)
    dx[pl.ds(empty, 2)] = jnp.zeros((2,) + dx.shape[1:], jnp.float32)
    for step in range(size):
        for plane in range(depth):
            slot = (pos ^ step) * depth + plane + start
            filter_columns(blocks[step], plane, own, weights, sx, dx, slot)
    for plane in range(extra):
        slot = (planes + 2) * front + plane
        filter_columns(boundary, plane, own, weights, sx, dx, slot)

    @pl.loop(0, own // TILE)
    def _(tile):
        first = pl.multiple_of(tile * TILE, TILE)
        total = render(sx, dx, first, planes - 2 + extra)
        if last:
            is_front = front == 1
            rest = tuple(other[channel, pl.ds(first, TILE), :] for channel in range(4))
            ahead = tuple(jnp.where(is_front, m, r) for m, r in zip(total, rest))
            behind = tuple(jnp.where(is_front, r, m) for m, r in zip(total, rest))
            v_sum, vt_sum, vu_sum, cover = over(ahead, behind)
            total = (0.5 * (v_sum + vu_sum), 0.5 * v_sum + 0.4 * vt_sum, 0.5 * (v_sum - vt_sum), cover)
        for channel in range(4):
            image[channel, pl.ds(first, TILE), :] = total[channel]


def edge_kernel(field, out):
    depth, height, width = field.shape
    lane = lax.broadcasted_iota(jnp.int32, (LANES, width), 1)
    count = depth * height // LANES
    for base in range(0, count, LANES // 4):
        packed = jnp.zeros((LANES, width), jnp.float32)
        for chunk in range(base, min(base + LANES // 4, count)):
            at = chunk * LANES
            rows = field[at // height, at % height : at % height + LANES, :]
            place = 4 * (chunk - base)
            packed = jnp.where(lane // 4 == chunk - base, pltpu.roll(rows, (place + 2) % width, 1), packed)
        out[base // (LANES // 4)] = jnp.transpose(packed)


def pack_kernel(size, info, field, before, after, *refs):
    outs, sides = refs[:-1], refs[-1]
    depth, height, width = field.shape
    own = outs[0].shape[1] - 16
    groups = height // own
    pos, front = info[0], info[1]
    row = lax.broadcasted_iota(jnp.int32, before.shape, 1) % 4
    left = jnp.where(info[2] == 1, before[...], 0.0)
    right = jnp.where(info[3] == 1, after[...], 0.0)
    sides[...] = jnp.where(row < 2, left, right).reshape(sides.shape)
    lane = lax.broadcasted_iota(jnp.int32, (4, LANES), 1)
    line = lax.broadcasted_iota(jnp.int32, (8, width), 0)

    def side_rows(plane, at, to):
        chunk = sides[pl.ds(plane * (4 * height // LANES) + at // LANES * 4, 4), :]
        return pltpu.roll(chunk, (to + LANES - at % LANES) % LANES, 1)

    for chunk in range(2):
        base = front * size if chunk == 0 else (1 - front) * size
        for step in range(size):
            out = outs[chunk * size + step]
            target = base + (pos ^ step)
            start = pl.multiple_of(target * own, 8)
            inner_top, inner_end = target > 0, target < groups - 1
            above = pl.multiple_of(jnp.maximum(start - 8, 0), 8)
            below = pl.multiple_of(jnp.minimum(start + own, height - 8), 8)
            for plane in range(depth):
                out[plane, 0:own, :] = field[plane, pl.ds(start, own), :]
                top = jnp.where(inner_top, pltpu.roll(field[plane, pl.ds(above, 8), :], 2, 0), 0.0)
                end = jnp.where(inner_end, pltpu.roll(field[plane, pl.ds(below, 8), :], 2, 0), 0.0)
                out[plane, own : own + 8, :] = jnp.where(line < 2, top, jnp.where(line < 4, end, 0.0))
                top = jnp.where(inner_top, side_rows(plane, jnp.maximum(start - 2, 0), 0), 0.0)
                end = jnp.where(inner_end, side_rows(plane, jnp.minimum(start + own, height - 2), 2), 0.0)
                out[plane, own + 8 : own + 12, :] = side_rows(plane, start, 0)
                out[plane, own + 12 : own + 16, :] = jnp.where(lane < 2, top, end)


def pick_kernel(size, info, *refs):
    blocks, out = refs[:size], refs[size]
    depth = blocks[0].shape[0]
    pos, front = info[0], info[1]
    count = 4 // depth
    for part in range(count):
        wanted = pos ^ (front * (size - count) + part)
        for step in range(size):

            @pl.when(wanted == step)
            def _():
                out[part * depth : (part + 1) * depth] = blocks[step][...]


SMEM = pl.BlockSpec(memory_space=pltpu.SMEM)
VMEM = pl.BlockSpec(memory_space=pltpu.VMEM)
PARAMS = pltpu.CompilerParams(vmem_limit_bytes=20 * 1024 * 1024)


def cost(flops, size):
    return pl.CostEstimate(flops=flops, bytes_accessed=size, transcendentals=0)


def local(field):
    groups = lax.axis_size("depth")
    columns = lax.axis_size("cols")
    size = groups // 2
    depth, height, width = field.shape
    own = height // groups
    me = lax.axis_index("depth")
    column = lax.axis_index("cols")
    has_left, has_right = column > 0, column < columns - 1
    info = jnp.stack([me % size, 1 - me // size, has_left, has_right]).astype(jnp.int32)
    weights = jnp.asarray(column_weights(width))
    f32 = jnp.float32
    block = jax.ShapeDtypeStruct((depth, own + 16, width), f32)
    image = jax.ShapeDtypeStruct((4, own, width), f32)

    edges = pl.pallas_call(
        edge_kernel,
        out_shape=jax.ShapeDtypeStruct((-(-depth * height // LANES // (LANES // 4)), LANES, LANES), f32),
        in_specs=[VMEM],
        out_specs=VMEM,
        compiler_params=PARAMS,
        name="edge_columns",
    )(field)
    if columns == 2:
        before = after = lax.ppermute(edges, "cols", [(0, 1), (1, 0)])
    else:
        before = lax.ppermute(edges, "cols", [(i, i + 1) for i in range(columns - 1)])
        after = lax.ppermute(edges, "cols", [(i + 1, i) for i in range(columns - 1)])
    blocks = pl.pallas_call(
        functools.partial(pack_kernel, size),
        out_shape=(block,) * (2 * size),
        in_specs=[SMEM] + [VMEM] * 3,
        out_specs=(VMEM,) * (2 * size),
        scratch_shapes=[pltpu.VMEM((edges.shape[0] * LANES, LANES), f32)],
        compiler_params=PARAMS,
        name="pack_blocks",
    )(info, field, before, after)

    def render_call(last):
        count = depth * size + (6 if last else 2)
        return pl.pallas_call(
            functools.partial(render_kernel, size, last),
            out_shape=image,
            in_specs=[SMEM] + [VMEM] * (size + (3 if last else 1)),
            out_specs=VMEM,
            scratch_shapes=[pltpu.VMEM((count, own + 16, width), f32)] * 2,
            compiler_params=PARAMS,
            cost_estimate=cost(5_000_000_000, 2_000_000),
            name="render_last" if last else "render_first",
        )

    pick = pl.pallas_call(
        functools.partial(pick_kernel, size),
        out_shape=jax.ShapeDtypeStruct((4,) + block.shape[1:], f32),
        in_specs=[SMEM] + [VMEM] * size,
        out_specs=VMEM,
        compiler_params=PARAMS,
        name="pick_boundary",
    )

    def swap(x, bits):
        return lax.ppermute(x, "depth", [(i, i ^ bits) for i in range(groups)])

    def gathered(mine):
        return [mine[0]] + [swap(mine[step], step) for step in range(1, size)]

    theirs = gathered(blocks[:size])
    boundary = swap(pick(info, *theirs), size)
    image_part = swap(render_call(False)(info, weights, *theirs), size)
    mine = gathered(blocks[size:])
    return render_call(True)(info, weights, *mine, boundary, image_part)


def solution(mesh):
    return jax.shard_map(
        local,
        mesh=mesh,
        in_specs=(P("depth", None, "cols"),),
        out_specs=P(None, "depth", "cols"),
        check_vma=False,
    )
```

```python
import functools
import math

import jax
import jax.numpy as jnp
import numpy as np
from jax import lax
from jax.experimental import pallas as pl
from jax.experimental.pallas import tpu as pltpu
from jax.sharding import PartitionSpec as P

GAUSS = (1.0, 4.0, 6.0, 4.0, 1.0)
DERIV = (-1.0, -2.0, 0.0, 2.0, 1.0)
SCALE = 7.0 / 4096.0
ONE = 49.0 / 256.0
HALF_LEN = math.sqrt(0.48 * 0.48 + 0.6 * 0.6 + 1.64 * 1.64)
SPEC = 0.35 / HALF_LEN**8
LOG2E = 1.0 / math.log(2.0)
LANES = 128
TILE = 16


def column_weights(width):
    body = np.zeros((width, 2 * width), np.float32)
    halo = np.zeros((4, 2 * width), np.float32)
    for out in range(width):
        for k in range(5):
            col = out - 2 + k
            for part, taps in enumerate((GAUSS, DERIV)):
                value = SCALE * taps[k]
                if 0 <= col < width:
                    body[col, part * width + out] = value
                else:
                    halo[col + 2 if col < 0 else col - width + 2, part * width + out] = value
    side = np.zeros((LANES, 2 * width), np.float32)
    for row in range(24):
        side[row] = halo[row % 4]
    return np.concatenate([body, body, body, side], 0).astype(jnp.bfloat16)


def three_parts(x):
    hi = x.astype(jnp.bfloat16)
    rest = x - hi.astype(jnp.float32)
    mid = rest.astype(jnp.bfloat16)
    lo = (rest - mid.astype(jnp.float32)).astype(jnp.bfloat16)
    return hi, mid, lo


def filter_columns(block, plane, own, weights, sx, dx, slot):
    width = block.shape[-1]
    hi, mid, lo = three_parts(block[plane, 0 : own + 8, :])
    sides = [part.astype(jnp.float32) for part in three_parts(block[plane, own + 8 : own + 16, :])]
    lanes_first = jnp.transpose(jnp.concatenate(sides, 0))
    inner = lax.broadcasted_iota(jnp.int32, lanes_first.shape, 1) % 8 < 4
    side = jnp.concatenate([jnp.where(inner, lanes_first, 0.0)[0:own], jnp.where(inner, 0.0, lanes_first)[0:8]], 0)
    side = jnp.concatenate([side, jnp.zeros((own + 8, LANES - side.shape[1]), jnp.float32)], 1)
    row = jnp.concatenate([hi, mid, lo, side.astype(jnp.bfloat16)], 1)
    both = jnp.dot(row, weights[...], preferred_element_type=jnp.float32)
    for out, part in ((sx, both[:, :width]), (dx, both[:, width:])):
        out[slot, 8 : 8 + own] = part[0:own]
        out[slot, 6:8] = part[own : own + 2]
        out[slot, 8 + own : 10 + own] = part[own + 2 : own + 4]


def gauss_rows(a, b, c, d, e):
    return (a + e) + 4.0 * (b + d) + 6.0 * c


def shade(t, gx, gy, gz, state):
    v_sum, vt_sum, vu_sum, cover = state
    opacity = 0.6 * pl.reciprocal(1.0 + jnp.exp2(jnp.minimum(13.2 * LOG2E - (6.0 * LOG2E) * t, 126.0)))
    tanh_t = jnp.tanh(t)
    tanh_u = jnp.tanh(t + 0.25)
    light = 0.48 * gx + 0.6 * gy + 0.64 * gz
    inv = lax.rsqrt(gx * gx + gy * gy + gz * gz + ONE)
    diffuse = jnp.maximum(light, 0.0) * inv
    half = jnp.maximum(light + gz, 0.0) * inv
    half = half * half
    half = half * half
    shading = 0.25 + 0.6 * diffuse + SPEC * (half * half)
    part = (1.0 - cover) * opacity
    value = part * shading
    return v_sum + value, vt_sum + value * tanh_t, vu_sum + value * tanh_u, cover + part


def render(sx, dx, first, count):
    def rows_of(ref, slot):
        return [ref[slot, pl.ds(first + 6 + k, TILE), :] for k in range(5)]

    zero = jnp.zeros((TILE, sx.shape[2]), jnp.float32)
    state = (zero, zero, zero, zero)
    chains = [[None] * 4 for _ in range(3)]
    for index in range(count + 4):
        a, b, c, d, e = rows_of(sx, index)
        inputs = [gauss_rows(a, b, c, d, e), (e - a) + 2.0 * (d - b), gauss_rows(*rows_of(dx, index))]
        totals, diff = [], None
        for which, (chain, x) in enumerate(zip(chains, inputs)):
            for level in range(4):
                before, chain[level] = chain[level], x
                if before is None:
                    x = None
                    break
                if which == 0 and level == 3:
                    diff = x - before
                x = x + before
            totals.append(x)
        if index >= 4:
            state = shade(totals[0], totals[2], totals[1], diff, state)
    return state


def over(front, back):
    rest = 1.0 - front[3]
    return tuple(f + rest * b for f, b in zip(front, back))


def render_kernel(size, last, info, weights, *refs):
    blocks, refs = refs[: size // 2], refs[size // 2 :]
    if last:
        boundary, other, image, sx, dx = refs
    else:
        image, sx, dx = refs
    depth, own = blocks[0].shape[0], image.shape[1]
    planes = depth * (size // 2)
    extra = 4 if last else 0
    chip, front = info[0], info[2]
    start = 2 * front + extra * (1 - front)
    empty = (1 - front) * (planes + extra)
    sx[pl.ds(empty, 2)] = jnp.zeros((2,) + sx.shape[1:], jnp.float32)
    dx[pl.ds(empty, 2)] = jnp.zeros((2,) + dx.shape[1:], jnp.float32)
    for step in range(size // 2):
        for plane in range(depth):
            slot = (chip ^ step) * depth + plane + start
            filter_columns(blocks[step], plane, own, weights, sx, dx, slot)
    for plane in range(extra):
        slot = (planes + 2) * front + plane
        filter_columns(boundary, plane, own, weights, sx, dx, slot)

    @pl.loop(0, own // TILE)
    def _(tile):
        first = pl.multiple_of(tile * TILE, TILE)
        total = render(sx, dx, first, planes - 2 + extra)
        if last:
            is_front = front == 1
            rest = tuple(other[channel, pl.ds(first, TILE), :] for channel in range(4))
            ahead = tuple(jnp.where(is_front, m, r) for m, r in zip(total, rest))
            behind = tuple(jnp.where(is_front, r, m) for m, r in zip(total, rest))
            v_sum, vt_sum, vu_sum, cover = over(ahead, behind)
            total = (0.5 * (v_sum + vu_sum), 0.5 * v_sum + 0.4 * vt_sum, 0.5 * (v_sum - vt_sum), cover)
        for channel in range(4):
            image[channel, pl.ds(first, TILE), :] = total[channel]


def edge_columns(field, out):
    depth, height, width = field.shape
    lane = lax.broadcasted_iota(jnp.int32, (LANES, width), 1)
    count = depth * height // LANES
    for base in range(0, count, LANES // 4):
        packed = jnp.zeros((LANES, width), jnp.float32)
        for chunk in range(base, min(base + LANES // 4, count)):
            at = chunk * LANES
            rows = field[at // height, at % height : at % height + LANES, :]
            place = 4 * (chunk - base)
            packed = jnp.where(lane // 4 == chunk - base, pltpu.roll(rows, (place + 2) % width, 1), packed)
        out[base // (LANES // 4)] = jnp.transpose(packed)


def rows_around(field, plane, target, own):
    height, width = field.shape[1:]
    line = lax.broadcasted_iota(jnp.int32, (8, width), 0)
    start = target * own
    above = pl.multiple_of(jnp.maximum(start - 8, 0), 8)
    below = pl.multiple_of(jnp.minimum(start + own, height - 8), 8)
    top = jnp.where(target > 0, pltpu.roll(field[plane, pl.ds(above, 8), :], 2, 0), 0.0)
    end = jnp.where(start + own < height, pltpu.roll(field[plane, pl.ds(below, 8), :], 2, 0), 0.0)
    return jnp.where(line < 2, top, jnp.where(line < 4, end, 0.0))


def targets(size, info):
    chip, core, front = info[0], info[1], info[2]
    for chunk in range(2):
        base = front * size if chunk == 0 else (1 - front) * size
        for step in range(size // 2):
            yield chunk * (size // 2) + step, base + 2 * (chip ^ step), core


def share_kernel(size, info, field, edges, share):
    own = share.shape[2] - 8
    edge_columns(field, edges)
    for index, target, core in targets(size, info):
        target = target + 1 - core
        for plane in range(field.shape[0]):
            start = pl.multiple_of(target * own, 8)
            share[index, plane, 0:own, :] = field[plane, pl.ds(start, own), :]
            share[index, plane, own : own + 8, :] = rows_around(field, plane, target, own)


def pack_kernel(size, info, field, shared, *refs):
    edges, outs, sides = refs[:4], refs[4:-1], refs[-1]
    depth, height, width = field.shape
    own = outs[0].shape[1] - 16
    row = lax.broadcasted_iota(jnp.int32, edges[0].shape, 1) % 4
    for which in range(2):
        left = jnp.where(info[3] == 1, edges[2 * which][...], 0.0)
        right = jnp.where(info[4] == 1, edges[2 * which + 1][...], 0.0)
        sides[which] = jnp.where(row < 2, left, right).reshape(sides.shape[1:])
    lane = lax.broadcasted_iota(jnp.int32, (4, LANES), 1)

    def side_rows(which, plane, at, to):
        chunk = sides[which, pl.ds(plane * (4 * height // LANES) + at // LANES * 4, 4), :]
        return pltpu.roll(chunk, (to + LANES - at % LANES) % LANES, 1)

    for index, target, core in targets(size, info):
        out = outs[index]
        target = target + core
        start = pl.multiple_of(target * own, 8)
        for which in range(2):
            for plane in range(depth):
                slot = (core if which == 0 else 1 - core) * depth + plane
                if which == 0:
                    out[slot, 0:own, :] = field[plane, pl.ds(start, own), :]
                    out[slot, own : own + 8, :] = rows_around(field, plane, target, own)
                else:
                    out[slot, 0 : own + 8, :] = shared[index, plane]
                top = side_rows(which, plane, jnp.maximum(start - 2, 0), 0)
                end = side_rows(which, plane, jnp.minimum(start + own, height - 2), 2)
                top = jnp.where(target > 0, top, 0.0)
                end = jnp.where(start + own < height, end, 0.0)
                out[slot, own + 8 : own + 12, :] = side_rows(which, plane, start, 0)
                out[slot, own + 12 : own + 16, :] = jnp.where(lane < 2, top, end)


def pick_kernel(size, info, *refs):
    blocks, out = refs[:-1], refs[-1]
    depth = blocks[0].shape[0]
    chip, front = info[0], info[2]
    count = 4 // depth
    for part in range(count):
        wanted = chip ^ (front * (size // 2 - count) + part)
        for step in range(size // 2):

            @pl.when(wanted == step)
            def _():
                out[part * depth : (part + 1) * depth] = blocks[step][...]


SMEM = pl.BlockSpec(memory_space=pltpu.SMEM)
VMEM = pl.BlockSpec(memory_space=pltpu.VMEM)
PARAMS = pltpu.CompilerParams(vmem_limit_bytes=20 * 1024 * 1024)


def cost(flops, size):
    return pl.CostEstimate(flops=flops, bytes_accessed=size, transcendentals=0)


def local(field):
    groups = lax.axis_size("depth")
    columns = lax.axis_size("cols")
    size = groups // 2
    depth, height, width = field.shape
    own = height // groups
    me = lax.axis_index("depth")
    column = lax.axis_index("cols")
    has_left, has_right = column > 0, column < columns - 1
    info = jnp.stack([me % size // 2, me % 2, 1 - me // size, has_left, has_right]).astype(jnp.int32)
    weights = jnp.asarray(column_weights(width))
    f32 = jnp.float32
    block = jax.ShapeDtypeStruct((2 * depth, own + 16, width), f32)
    image = jax.ShapeDtypeStruct((4, own, width), f32)
    edge_groups = -(-depth * height // LANES // (LANES // 4))

    edges, share = pl.pallas_call(
        functools.partial(share_kernel, size),
        out_shape=(
            jax.ShapeDtypeStruct((edge_groups, LANES, LANES), f32),
            jax.ShapeDtypeStruct((size, depth, own + 8, width), f32),
        ),
        in_specs=[SMEM, VMEM],
        out_specs=(VMEM, VMEM),
        compiler_params=PARAMS,
        name="share_with_core",
    )(info, field)
    shared = lax.ppermute(share, "depth", [(i, i ^ 1) for i in range(groups)])

    def from_column(flip, shifts):
        route = []
        for i in range(groups):
            for j in range(columns):
                for shift in shifts:
                    if 0 <= j + shift < columns:
                        route.append((i * columns + j, (i ^ flip) * columns + j + shift))
        return lax.ppermute(edges, ("depth", "cols"), route)

    sides = []
    for flip in range(2):
        if columns == 2:
            sides += [from_column(flip, (-1, 1))] * 2
        else:
            sides += [from_column(flip, (1,)), from_column(flip, (-1,))]
    blocks = pl.pallas_call(
        functools.partial(pack_kernel, size),
        out_shape=(block,) * size,
        in_specs=[SMEM] + [VMEM] * 6,
        out_specs=(VMEM,) * size,
        scratch_shapes=[pltpu.VMEM((2, edge_groups * LANES, LANES), f32)],
        compiler_params=PARAMS,
        name="pack_blocks",
    )(info, field, shared, *sides)

    def render_call(last):
        count = depth * size + (6 if last else 2)
        return pl.pallas_call(
            functools.partial(render_kernel, size, last),
            out_shape=image,
            in_specs=[SMEM] + [VMEM] * (size // 2 + (3 if last else 1)),
            out_specs=VMEM,
            scratch_shapes=[pltpu.VMEM((count, own + 16, width), f32)] * 2,
            compiler_params=PARAMS,
            cost_estimate=cost(5_000_000_000, 2_000_000),
            name="render_last" if last else "render_first",
        )

    pick = pl.pallas_call(
        functools.partial(pick_kernel, size),
        out_shape=jax.ShapeDtypeStruct((4,) + block.shape[1:], f32),
        in_specs=[SMEM] + [VMEM] * (size // 2),
        out_specs=VMEM,
        compiler_params=PARAMS,
        name="pick_boundary",
    )

    def swap(x, bits):
        return lax.ppermute(x, "depth", [(i, i ^ bits) for i in range(groups)])

    def gathered(mine):
        return [mine[0]] + [swap(mine[step], 2 * step) for step in range(1, size // 2)]

    theirs = gathered(blocks[: size // 2])
    boundary = swap(pick(info, *theirs), size)
    image_part = swap(render_call(False)(info, weights, *theirs), size)
    mine = gathered(blocks[size // 2 :])
    return render_call(True)(info, weights, *mine, boundary, image_part)


def solution(mesh):
    return jax.shard_map(
        local,
        mesh=mesh,
        in_specs=(P("depth", None, "cols"),),
        out_specs=P(None, "depth", "cols"),
        check_vma=False,
    )
```

```python
import functools
import math

import jax
import jax.numpy as jnp
import numpy as np
from jax import lax
from jax.experimental import pallas as pl
from jax.experimental.pallas import tpu as pltpu
from jax.sharding import PartitionSpec as P

GAUSS = (1.0, 4.0, 6.0, 4.0, 1.0)
DERIV = (-1.0, -2.0, 0.0, 2.0, 1.0)
SCALE = 7.0 / 4096.0
ONE = 49.0 / 256.0
HALF_LEN = math.sqrt(0.48 * 0.48 + 0.6 * 0.6 + 1.64 * 1.64)
SPEC = 0.35 / HALF_LEN**8
LOG2E = 1.0 / math.log(2.0)
LANES = 128
TILE = 16


def column_weights(width):
    body = np.zeros((width, 2 * width), np.float32)
    halo = np.zeros((4, 2 * width), np.float32)
    for out in range(width):
        for k in range(5):
            col = out - 2 + k
            for part, taps in enumerate((GAUSS, DERIV)):
                value = SCALE * taps[k]
                if 0 <= col < width:
                    body[col, part * width + out] = value
                else:
                    halo[col + 2 if col < 0 else col - width + 2, part * width + out] = value
    side = np.zeros((LANES, 2 * width), np.float32)
    for row in range(24):
        side[row] = halo[row % 4]
    return np.concatenate([body, body, body, side], 0).astype(jnp.bfloat16)


def three_parts(x):
    hi = x.astype(jnp.bfloat16)
    rest = x - hi.astype(jnp.float32)
    mid = rest.astype(jnp.bfloat16)
    lo = (rest - mid.astype(jnp.float32)).astype(jnp.bfloat16)
    return hi, mid, lo


def filter_columns(block, plane, own, weights, sx, dx, slot):
    width = block.shape[-1]
    hi, mid, lo = three_parts(block[plane, 0 : own + 8, :])
    sides = [part.astype(jnp.float32) for part in three_parts(block[plane, own + 8 : own + 16, :])]
    lanes_first = jnp.transpose(jnp.concatenate(sides, 0))
    inner = lax.broadcasted_iota(jnp.int32, lanes_first.shape, 1) % 8 < 4
    side = jnp.concatenate([jnp.where(inner, lanes_first, 0.0)[0:own], jnp.where(inner, 0.0, lanes_first)[0:8]], 0)
    side = jnp.concatenate([side, jnp.zeros((own + 8, LANES - side.shape[1]), jnp.float32)], 1)
    row = jnp.concatenate([hi, mid, lo, side.astype(jnp.bfloat16)], 1)
    both = jnp.dot(row, weights[...], preferred_element_type=jnp.float32)
    for out, part in ((sx, both[:, :width]), (dx, both[:, width:])):
        out[slot, 8 : 8 + own] = part[0:own]
        out[slot, 6:8] = part[own : own + 2]
        out[slot, 8 + own : 10 + own] = part[own + 2 : own + 4]


def gauss_rows(a, b, c, d, e):
    return (a + e) + 4.0 * (b + d) + 6.0 * c


def shade(t, gx, gy, gz, state):
    v_sum, vt_sum, vu_sum, cover = state
    opacity = 0.6 * pl.reciprocal(1.0 + jnp.exp2(jnp.minimum(13.2 * LOG2E - (6.0 * LOG2E) * t, 126.0)))
    tanh_t = jnp.tanh(t)
    tanh_u = jnp.tanh(t + 0.25)
    light = 0.48 * gx + 0.6 * gy + 0.64 * gz
    inv = lax.rsqrt(gx * gx + gy * gy + gz * gz + ONE)
    diffuse = jnp.maximum(light, 0.0) * inv
    half = jnp.maximum(light + gz, 0.0) * inv
    half = half * half
    half = half * half
    shading = 0.25 + 0.6 * diffuse + SPEC * (half * half)
    part = (1.0 - cover) * opacity
    value = part * shading
    return v_sum + value, vt_sum + value * tanh_t, vu_sum + value * tanh_u, cover + part


def render(sx, dx, first, count):
    def rows_of(ref, slot):
        return [ref[slot, pl.ds(first + 6 + k, TILE), :] for k in range(5)]

    zero = jnp.zeros((TILE, sx.shape[2]), jnp.float32)
    state = (zero, zero, zero, zero)
    chains = [[None] * 4 for _ in range(3)]
    for index in range(count + 4):
        a, b, c, d, e = rows_of(sx, index)
        inputs = [gauss_rows(a, b, c, d, e), (e - a) + 2.0 * (d - b), gauss_rows(*rows_of(dx, index))]
        totals, diff = [], None
        for which, (chain, x) in enumerate(zip(chains, inputs)):
            for level in range(4):
                before, chain[level] = chain[level], x
                if before is None:
                    x = None
                    break
                if which == 0 and level == 3:
                    diff = x - before
                x = x + before
            totals.append(x)
        if index >= 4:
            state = shade(totals[0], totals[2], totals[1], diff, state)
    return state


def over(front, back):
    rest = 1.0 - front[3]
    return tuple(f + rest * b for f, b in zip(front, back))


def render_kernel(size, last, info, weights, *refs):
    blocks, refs = refs[: size // 2], refs[size // 2 :]
    if last:
        boundary, image, sx, dx = refs
    else:
        image, sx, dx = refs
    depth, own = blocks[0].shape[0], image.shape[1]
    planes = depth * (size // 2)
    extra = 4 if last else 0
    chip, front = info[0], info[2]
    start = 2 * front + extra * (1 - front)
    empty = (1 - front) * (planes + extra)
    sx[pl.ds(empty, 2)] = jnp.zeros((2,) + sx.shape[1:], jnp.float32)
    dx[pl.ds(empty, 2)] = jnp.zeros((2,) + dx.shape[1:], jnp.float32)
    for step in range(size // 2):
        for plane in range(depth):
            slot = (chip ^ step) * depth + plane + start
            filter_columns(blocks[step], plane, own, weights, sx, dx, slot)
    if last:
        for plane in range(extra):
            slot = (planes + 2) * front + plane
            filter_columns(boundary, plane, own, weights, sx, dx, slot)

    @pl.loop(0, own // TILE)
    def _(tile):
        first = pl.multiple_of(tile * TILE, TILE)
        total = render(sx, dx, first, planes - 2 + extra)
        for channel in range(4):
            image[channel, pl.ds(first, TILE), :] = total[channel]


def join_kernel(info, mine, other, picture):
    is_front = info[2] == 1
    mine = tuple(mine[channel] for channel in range(4))
    other = tuple(other[channel] for channel in range(4))
    ahead = tuple(jnp.where(is_front, m, o) for m, o in zip(mine, other))
    behind = tuple(jnp.where(is_front, o, m) for m, o in zip(mine, other))
    v_sum, vt_sum, vu_sum, cover = over(ahead, behind)
    picture[0] = 0.5 * (v_sum + vu_sum)
    picture[1] = 0.5 * v_sum + 0.4 * vt_sum
    picture[2] = 0.5 * (v_sum - vt_sum)
    picture[3] = cover


def edge_columns(field, out):
    depth, height, width = field.shape
    lane = lax.broadcasted_iota(jnp.int32, (LANES, width), 1)
    count = depth * height // LANES
    for base in range(0, count, LANES // 4):
        packed = jnp.zeros((LANES, width), jnp.float32)
        for chunk in range(base, min(base + LANES // 4, count)):
            at = chunk * LANES
            rows = field[at // height, at % height : at % height + LANES, :]
            place = 4 * (chunk - base)
            packed = jnp.where(lane // 4 == chunk - base, pltpu.roll(rows, (place + 2) % width, 1), packed)
        out[base // (LANES // 4)] = jnp.transpose(packed)


def rows_around(field, plane, target, own):
    height, width = field.shape[1:]
    line = lax.broadcasted_iota(jnp.int32, (8, width), 0)
    start = target * own
    above = pl.multiple_of(jnp.maximum(start - 8, 0), 8)
    below = pl.multiple_of(jnp.minimum(start + own, height - 8), 8)
    top = jnp.where(target > 0, pltpu.roll(field[plane, pl.ds(above, 8), :], 2, 0), 0.0)
    end = jnp.where(start + own < height, pltpu.roll(field[plane, pl.ds(below, 8), :], 2, 0), 0.0)
    return jnp.where(line < 2, top, jnp.where(line < 4, end, 0.0))


def targets(size, info):
    chip, core, front = info[0], info[1], info[2]
    for chunk in range(2):
        base = front * size if chunk == 0 else (1 - front) * size
        for step in range(size // 2):
            yield chunk * (size // 2) + step, base + 2 * (chip ^ step), core


def pack_kernel(size, info, field, shared, *refs):
    edges, outs, sides = refs[:4], refs[4:-1], refs[-1]
    depth, height, width = field.shape
    own = outs[0].shape[1] - 16
    row = lax.broadcasted_iota(jnp.int32, edges[0].shape, 1) % 4
    for which in range(2):
        left = jnp.where(info[3] == 1, edges[2 * which][...], 0.0)
        right = jnp.where(info[4] == 1, edges[2 * which + 1][...], 0.0)
        sides[which] = jnp.where(row < 2, left, right).reshape(sides.shape[1:])
    lane = lax.broadcasted_iota(jnp.int32, (4, LANES), 1)

    def side_rows(which, plane, at, to):
        chunk = sides[which, pl.ds(plane * (4 * height // LANES) + at // LANES * 4, 4), :]
        return pltpu.roll(chunk, (to + LANES - at % LANES) % LANES, 1)

    for index, target, core in targets(size, info):
        out = outs[index]
        target = target + core
        start = pl.multiple_of(target * own, 8)
        for which in range(2):
            for plane in range(depth):
                slot = (core if which == 0 else 1 - core) * depth + plane
                source = (field, shared)[which]
                out[slot, 0:own, :] = source[plane, pl.ds(start, own), :]
                out[slot, own : own + 8, :] = rows_around(source, plane, target, own)
                top = side_rows(which, plane, jnp.maximum(start - 2, 0), 0)
                end = side_rows(which, plane, jnp.minimum(start + own, height - 2), 2)
                top = jnp.where(target > 0, top, 0.0)
                end = jnp.where(start + own < height, end, 0.0)
                out[slot, own + 8 : own + 12, :] = side_rows(which, plane, start, 0)
                out[slot, own + 12 : own + 16, :] = jnp.where(lane < 2, top, end)


def pick_kernel(size, info, *refs):
    blocks, out = refs[:-1], refs[-1]
    depth = blocks[0].shape[0]
    chip, front = info[0], info[2]
    count = 4 // depth
    for part in range(count):
        wanted = chip ^ (front * (size // 2 - count) + part)
        for step in range(size // 2):

            @pl.when(wanted == step)
            def _():
                out[part * depth : (part + 1) * depth] = blocks[step][...]


SMEM = pl.BlockSpec(memory_space=pltpu.SMEM)
VMEM = pl.BlockSpec(memory_space=pltpu.VMEM)
PARAMS = pltpu.CompilerParams(vmem_limit_bytes=20 * 1024 * 1024)


def cost(flops, size):
    return pl.CostEstimate(flops=flops, bytes_accessed=size, transcendentals=0)


def local(field):
    groups = lax.axis_size("depth")
    columns = lax.axis_size("cols")
    size = groups // 2
    depth, height, width = field.shape
    own = height // groups
    me = lax.axis_index("depth")
    column = lax.axis_index("cols")
    has_left, has_right = column > 0, column < columns - 1
    info = jnp.stack([me % size // 2, me % 2, 1 - me // size, has_left, has_right]).astype(jnp.int32)
    weights = jnp.asarray(column_weights(width))
    f32 = jnp.float32
    block = jax.ShapeDtypeStruct((2 * depth, own + 16, width), f32)
    image = jax.ShapeDtypeStruct((4, own, width), f32)
    edge_groups = -(-depth * height // LANES // (LANES // 4))

    shared = lax.ppermute(field, "depth", [(i, i ^ 1) for i in range(groups)])
    edges = pl.pallas_call(
        edge_columns,
        out_shape=jax.ShapeDtypeStruct((edge_groups, LANES, LANES), f32),
        in_specs=[VMEM],
        out_specs=VMEM,
        compiler_params=PARAMS,
        name="edge_columns",
    )(field)

    def from_column(flip, shifts):
        route = []
        for i in range(groups):
            for j in range(columns):
                for shift in shifts:
                    if 0 <= j + shift < columns:
                        route.append((i * columns + j, (i ^ flip) * columns + j + shift))
        return lax.ppermute(edges, ("depth", "cols"), route)

    sides = []
    for flip in range(2):
        if columns == 2:
            sides += [from_column(flip, (-1, 1))] * 2
        else:
            sides += [from_column(flip, (1,)), from_column(flip, (-1,))]
    blocks = pl.pallas_call(
        functools.partial(pack_kernel, size),
        out_shape=(block,) * size,
        in_specs=[SMEM] + [VMEM] * 6,
        out_specs=(VMEM,) * size,
        scratch_shapes=[pltpu.VMEM((2, edge_groups * LANES, LANES), f32)],
        compiler_params=PARAMS,
        name="pack_blocks",
    )(info, field, shared, *sides)

    def render_call(last):
        count = depth * size + (6 if last else 2)
        return pl.pallas_call(
            functools.partial(render_kernel, size, last),
            out_shape=image,
            in_specs=[SMEM] + [VMEM] * (1 + size // 2 + (1 if last else 0)),
            out_specs=VMEM,
            scratch_shapes=[pltpu.VMEM((count, own + 16, width), f32)] * 2,
            compiler_params=PARAMS,
            cost_estimate=cost(5_000_000_000, 2_000_000),
            name="render_last" if last else "render_first",
        )

    pick = pl.pallas_call(
        functools.partial(pick_kernel, size),
        out_shape=jax.ShapeDtypeStruct((4,) + block.shape[1:], f32),
        in_specs=[SMEM] + [VMEM] * (size // 2),
        out_specs=VMEM,
        compiler_params=PARAMS,
        name="pick_boundary",
    )

    def swap(x, bits):
        return lax.ppermute(x, "depth", [(i, i ^ bits) for i in range(groups)])

    def gathered(mine):
        return [mine[0]] + [swap(mine[step], 2 * step) for step in range(1, size // 2)]

    theirs = gathered(blocks[: size // 2])
    boundary = swap(pick(info, *theirs), size)
    image_part = swap(render_call(False)(info, weights, *theirs), size)
    mine = [blocks[size // 2]]
    for step in range(1, size // 2):
        held, _ = lax.optimization_barrier((blocks[size // 2 + step], theirs[step]))
        mine.append(swap(held, 2 * step))
    own_part = render_call(True)(info, weights, *mine, boundary)
    return pl.pallas_call(
        join_kernel,
        out_shape=image,
        in_specs=[SMEM, VMEM, VMEM],
        out_specs=VMEM,
        compiler_params=PARAMS,
        name="join_halves",
    )(info, own_part, image_part)


def solution(mesh):
    return jax.shard_map(
        local,
        mesh=mesh,
        in_specs=(P("depth", None, "cols"),),
        out_specs=P(None, "depth", "cols"),
        check_vma=False,
    )
```

```python
import functools
import math

import jax
import jax.numpy as jnp
import numpy as np
from jax import lax
from jax.experimental import pallas as pl
from jax.experimental.pallas import tpu as pltpu
from jax.sharding import PartitionSpec as P

GAUSS = (1.0, 4.0, 6.0, 4.0, 1.0)
DERIV = (-1.0, -2.0, 0.0, 2.0, 1.0)
SCALE = 7.0 / 4096.0
ONE = 49.0 / 256.0
HALF_LEN = math.sqrt(0.48 * 0.48 + 0.6 * 0.6 + 1.64 * 1.64)
SPEC = 0.35 / HALF_LEN**8
LOG2E = 1.0 / math.log(2.0)
LANES = 128
TILE = 16


def column_weights(width):
    body = np.zeros((width, 2 * width), np.float32)
    halo = np.zeros((4, 2 * width), np.float32)
    for out in range(width):
        for k in range(5):
            col = out - 2 + k
            for part, taps in enumerate((GAUSS, DERIV)):
                value = SCALE * taps[k]
                if 0 <= col < width:
                    body[col, part * width + out] = value
                else:
                    halo[col + 2 if col < 0 else col - width + 2, part * width + out] = value
    side = np.zeros((LANES, 2 * width), np.float32)
    for row in range(24):
        side[row] = halo[row % 4]
    return np.concatenate([body, body, body, side], 0).astype(jnp.bfloat16)


def three_parts(x):
    hi = x.astype(jnp.bfloat16)
    rest = x - hi.astype(jnp.float32)
    mid = rest.astype(jnp.bfloat16)
    lo = (rest - mid.astype(jnp.float32)).astype(jnp.bfloat16)
    return hi, mid, lo


def filter_columns(block, plane, side, own, weights, sx, dx, slot):
    width = block.shape[-1]
    hi, mid, lo = three_parts(block[plane])
    sides = [part.astype(jnp.float32) for part in three_parts(side)]
    lanes_first = jnp.transpose(jnp.concatenate(sides, 0))
    inner = lax.broadcasted_iota(jnp.int32, lanes_first.shape, 1) % 8 < 4
    halo = jnp.concatenate([jnp.where(inner, lanes_first, 0.0)[0:own], jnp.where(inner, 0.0, lanes_first)[0:8]], 0)
    halo = jnp.concatenate([halo, jnp.zeros((own + 8, LANES - halo.shape[1]), jnp.float32)], 1)
    row = jnp.concatenate([hi, mid, lo, halo.astype(jnp.bfloat16)], 1)
    both = jnp.dot(row, weights[...], preferred_element_type=jnp.float32)
    for out, part in ((sx, both[:, :width]), (dx, both[:, width:])):
        out[slot, 8 : 8 + own] = part[0:own]
        out[slot, 6:8] = part[own : own + 2]
        out[slot, 8 + own : 10 + own] = part[own + 2 : own + 4]


def gauss_rows(a, b, c, d, e):
    return (a + e) + 4.0 * (b + d) + 6.0 * c


def shade(t, gx, gy, gz, state):
    v_sum, vt_sum, vu_sum, cover = state
    opacity = 0.6 * pl.reciprocal(1.0 + jnp.exp2(jnp.minimum(13.2 * LOG2E - (6.0 * LOG2E) * t, 126.0)))
    tanh_t = jnp.tanh(t)
    tanh_u = jnp.tanh(t + 0.25)
    light = 0.48 * gx + 0.6 * gy + 0.64 * gz
    inv = lax.rsqrt(gx * gx + gy * gy + gz * gz + ONE)
    diffuse = jnp.maximum(light, 0.0) * inv
    half = jnp.maximum(light + gz, 0.0) * inv
    half = half * half
    half = half * half
    shading = 0.25 + 0.6 * diffuse + SPEC * (half * half)
    part = (1.0 - cover) * opacity
    value = part * shading
    return v_sum + value, vt_sum + value * tanh_t, vu_sum + value * tanh_u, cover + part


def render(sx, dx, first, count):
    def rows_of(ref, slot):
        return [ref[slot, pl.ds(first + 6 + k, TILE), :] for k in range(5)]

    zero = jnp.zeros((TILE, sx.shape[2]), jnp.float32)
    state = (zero, zero, zero, zero)
    chains = [[None] * 4 for _ in range(3)]
    for index in range(count + 4):
        a, b, c, d, e = rows_of(sx, index)
        inputs = [gauss_rows(a, b, c, d, e), (e - a) + 2.0 * (d - b), gauss_rows(*rows_of(dx, index))]
        totals, diff = [], None
        for which, (chain, x) in enumerate(zip(chains, inputs)):
            for level in range(4):
                before, chain[level] = chain[level], x
                if before is None:
                    x = None
                    break
                if which == 0 and level == 3:
                    diff = x - before
                x = x + before
            totals.append(x)
        if index >= 4:
            state = shade(totals[0], totals[2], totals[1], diff, state)
    return state


def over(front, back):
    rest = 1.0 - front[3]
    return tuple(f + rest * b for f, b in zip(front, back))


def render_kernel(size, last, info, weights, before, after, *refs):
    steps = size // 2
    blocks, (image, sx, dx) = refs[:-3], refs[-3:]
    depth, own = blocks[0].shape[0], image.shape[1]
    planes = depth * steps
    extra = 4 if last else 0
    chip, front = info[0], info[2]
    start = 2 * front + extra * (1 - front)
    empty = (1 - front) * (planes + extra)
    sx[pl.ds(empty, 2)] = jnp.zeros((2,) + sx.shape[1:], jnp.float32)
    dx[pl.ds(empty, 2)] = jnp.zeros((2,) + dx.shape[1:], jnp.float32)
    line = lax.broadcasted_iota(jnp.int32, (8, LANES), 0) % 4
    from_left = (line < 2) & (info[3] == 1)
    from_right = (line >= 2) & (info[4] == 1)

    def side(index):
        left, right = (
            jnp.concatenate([ref[0, 4 * index : 4 * index + 4], ref[1, 4 * index : 4 * index + 4]], 0)
            for ref in (before, after)
        )
        return jnp.where(from_left, left, jnp.where(from_right, right, 0.0))

    for step in range(steps):
        for plane in range(depth):
            slot = (chip ^ step) * depth + plane + start
            filter_columns(blocks[step], plane, side(step * depth + plane), own, weights, sx, dx, slot)
    for plane in range(extra):
        slot = (planes + 2) * front + plane
        filter_columns(blocks[steps], plane, side(planes + plane), own, weights, sx, dx, slot)

    @pl.loop(0, own // TILE)
    def _(tile):
        first = pl.multiple_of(tile * TILE, TILE)
        total = render(sx, dx, first, planes - 2 + extra)
        for channel in range(4):
            image[channel, pl.ds(first, TILE), :] = total[channel]


def join_kernel(info, mine, other, picture):
    is_front = info[2] == 1
    mine = tuple(mine[channel] for channel in range(4))
    other = tuple(other[channel] for channel in range(4))
    ahead = tuple(jnp.where(is_front, m, o) for m, o in zip(mine, other))
    behind = tuple(jnp.where(is_front, o, m) for m, o in zip(mine, other))
    v_sum, vt_sum, vu_sum, cover = over(ahead, behind)
    picture[0] = 0.5 * (v_sum + vu_sum)
    picture[1] = 0.5 * v_sum + 0.4 * vt_sum
    picture[2] = 0.5 * (v_sum - vt_sum)
    picture[3] = cover


def edge_kernel(*refs):
    blocks, out = refs[:-1], refs[-1]
    own, width = blocks[0].shape[1] - 8, blocks[0].shape[2]
    places = [(block, plane) for block in blocks for plane in range(block.shape[0])]
    group = LANES // 4
    lane = lax.broadcasted_iota(jnp.int32, (own + 8, width), 1) // 4
    for base in range(0, len(places), group):
        packed = jnp.zeros((own + 8, width), jnp.float32)
        for at, (block, plane) in enumerate(places[base : base + group]):
            packed = jnp.where(lane == at, pltpu.roll(block[plane], (4 * at + 2) % width, 1), packed)
        for part, rows in enumerate((packed[0:own], packed[own:])):
            missing = LANES - rows.shape[0]
            if missing:
                rows = jnp.concatenate([rows, jnp.zeros((missing, width), jnp.float32)], 0)
            out[part, 4 * base : 4 * base + LANES] = jnp.transpose(rows)


def rows_around(field, plane, target, own):
    height, width = field.shape[1:]
    line = lax.broadcasted_iota(jnp.int32, (8, width), 0)
    start = target * own
    above = pl.multiple_of(jnp.maximum(start - 8, 0), 8)
    below = pl.multiple_of(jnp.minimum(start + own, height - 8), 8)
    top = jnp.where(target > 0, pltpu.roll(field[plane, pl.ds(above, 8), :], 2, 0), 0.0)
    end = jnp.where(start + own < height, pltpu.roll(field[plane, pl.ds(below, 8), :], 2, 0), 0.0)
    return jnp.where(line < 2, top, jnp.where(line < 4, end, 0.0))


def targets(size, info):
    chip, core, front = info[0], info[1], info[2]
    for chunk in range(2):
        base = front * size if chunk == 0 else (1 - front) * size
        for step in range(size // 2):
            yield chunk * (size // 2) + step, base + 2 * (chip ^ step), core


def pack_kernel(size, shared, info, source, *refs):
    outs = refs[-size:]
    depth, own = source.shape[0], outs[0].shape[1] - 8
    for index, target, core in targets(size, info):
        target = target + core
        start = pl.multiple_of(target * own, 8)
        for plane in range(depth):
            slot = (1 - core if shared else core) * depth + plane
            outs[index][slot, 0:own, :] = source[plane, pl.ds(start, own), :]
            outs[index][slot, own : own + 8, :] = rows_around(source, plane, target, own)


def pick_kernel(size, info, *refs):
    blocks, out = refs[:-1], refs[-1]
    depth = blocks[0].shape[0]
    chip, front = info[0], info[2]
    count = 4 // depth
    for part in range(count):
        wanted = chip ^ (front * (size // 2 - count) + part)
        for step in range(size // 2):

            @pl.when(wanted == step)
            def _():
                out[part * depth : (part + 1) * depth] = blocks[step][...]


SMEM = pl.BlockSpec(memory_space=pltpu.SMEM)
VMEM = pl.BlockSpec(memory_space=pltpu.VMEM)
PARAMS = pltpu.CompilerParams(vmem_limit_bytes=20 * 1024 * 1024)


def cost(flops, size):
    return pl.CostEstimate(flops=flops, bytes_accessed=size, transcendentals=0)


def local(field):
    groups = lax.axis_size("depth")
    columns = lax.axis_size("cols")
    size = groups // 2
    depth, height, width = field.shape
    own = height // groups
    me = lax.axis_index("depth")
    column = lax.axis_index("cols")
    has_left, has_right = column > 0, column < columns - 1
    info = jnp.stack([me % size // 2, me % 2, 1 - me // size, has_left, has_right]).astype(jnp.int32)
    weights = jnp.asarray(column_weights(width))
    f32 = jnp.float32
    steps = size // 2
    block = jax.ShapeDtypeStruct((2 * depth, own + 8, width), f32)
    image = jax.ShapeDtypeStruct((4, own, width), f32)

    shared = lax.ppermute(field, "depth", [(i, i ^ 1) for i in range(groups)])
    blocks = ()
    for source in (field, shared):
        blocks = pl.pallas_call(
            functools.partial(pack_kernel, size, source is shared),
            out_shape=(block,) * size,
            in_specs=[SMEM, VMEM] + [VMEM] * len(blocks),
            out_specs=(VMEM,) * size,
            input_output_aliases={2 + i: i for i in range(len(blocks))},
            compiler_params=PARAMS,
            name="pack_shared" if source is shared else "pack_own",
        )(info, source, *blocks)

    def columns_near(parts):
        count = sum(part.shape[0] for part in parts)
        edges = pl.pallas_call(
            edge_kernel,
            out_shape=jax.ShapeDtypeStruct((2, -(-count // (LANES // 4)) * LANES, LANES), f32),
            in_specs=[VMEM] * len(parts),
            out_specs=VMEM,
            compiler_params=PARAMS,
            cost_estimate=cost(1000, 1000),
            name="edge_columns",
        )(*parts)
        if columns == 2:
            return (lax.ppermute(edges, "cols", [(0, 1), (1, 0)]),) * 2
        return tuple(
            lax.ppermute(edges, "cols", [(i, i + shift) for i in range(columns) if 0 <= i + shift < columns])
            for shift in (1, -1)
        )

    def render_call(last, parts):
        count = depth * size + (6 if last else 2)
        return pl.pallas_call(
            functools.partial(render_kernel, size, last),
            out_shape=image,
            in_specs=[SMEM] + [VMEM] * (3 + len(parts)),
            out_specs=VMEM,
            scratch_shapes=[pltpu.VMEM((count, own + 16, width), f32)] * 2,
            compiler_params=PARAMS,
            cost_estimate=cost(1000, 1000),
            name="render_last" if last else "render_first",
        )(info, weights, *columns_near(parts), *parts)

    pick = pl.pallas_call(
        functools.partial(pick_kernel, size),
        out_shape=jax.ShapeDtypeStruct((4,) + block.shape[1:], f32),
        in_specs=[SMEM] + [VMEM] * (size // 2),
        out_specs=VMEM,
        compiler_params=PARAMS,
        cost_estimate=cost(1000, 1000),
        name="pick_boundary",
    )

    def swap(x, bits):
        return lax.ppermute(x, "depth", [(i, i ^ bits) for i in range(groups)])

    def gathered(parts):
        return [parts[0]] + [swap(parts[step], 2 * step) for step in range(1, steps)]

    theirs = gathered(blocks[:steps])
    boundary = swap(pick(info, *theirs), size)
    first_image = render_call(False, theirs)
    image_part = swap(first_image, size)
    mine = [blocks[steps]]
    for step in range(1, steps):
        held, _ = lax.optimization_barrier((blocks[steps + step], theirs[step]))
        mine.append(swap(held, 2 * step))
    parts, _ = lax.optimization_barrier((mine + [boundary], first_image))
    own_part = render_call(True, parts)
    return pl.pallas_call(
        join_kernel,
        out_shape=image,
        in_specs=[SMEM, VMEM, VMEM],
        out_specs=VMEM,
        compiler_params=PARAMS,
        cost_estimate=cost(1000, 1000),
        name="join_halves",
    )(info, own_part, image_part)


def solution(mesh):
    return jax.shard_map(
        local,
        mesh=mesh,
        in_specs=(P("depth", None, "cols"),),
        out_specs=P(None, "depth", "cols"),
        check_vma=False,
    )
```

```python
import functools
import math

import jax
import jax.numpy as jnp
import numpy as np
from jax import lax
from jax.experimental import pallas as pl
from jax.experimental.pallas import tpu as pltpu
from jax.sharding import PartitionSpec as P

GAUSS = (1.0, 4.0, 6.0, 4.0, 1.0)
DERIV = (-1.0, -2.0, 0.0, 2.0, 1.0)
SCALE = 7.0 / 4096.0
ONE = 49.0 / 256.0
HALF_LEN = math.sqrt(0.48 * 0.48 + 0.6 * 0.6 + 1.64 * 1.64)
SPEC = 0.35 / HALF_LEN**8
LOG2E = 1.0 / math.log(2.0)
LANES = 128
TILE = 16


def column_weights(width):
    body = np.zeros((width, 2 * width), np.float32)
    for out in range(width):
        for k in range(5):
            if 0 <= out - 2 + k < width:
                body[out - 2 + k, out] = SCALE * GAUSS[k]
                body[out - 2 + k, width + out] = SCALE * DERIV[k]
    return np.concatenate([body, body, body], 0).astype(jnp.bfloat16)


def three_parts(x):
    hi = x.astype(jnp.bfloat16)
    rest = x - hi.astype(jnp.float32)
    mid = rest.astype(jnp.bfloat16)
    lo = (rest - mid.astype(jnp.float32)).astype(jnp.bfloat16)
    return hi, mid, lo


def filter_columns(block, plane, own, weights, sx, dx, slot):
    width = block.shape[-1]
    row = jnp.concatenate(three_parts(block[plane]), 1)
    both = jnp.dot(row, weights[...], preferred_element_type=jnp.float32)
    for out, part in ((sx, both[:, :width]), (dx, both[:, width:])):
        out[slot, 8 : 8 + own] = part[0:own]
        out[slot, 6:8] = part[own : own + 2]
        out[slot, 8 + own : 10 + own] = part[own + 2 : own + 4]


def gauss_rows(a, b, c, d, e):
    return (a + e) + 4.0 * (b + d) + 6.0 * c


def shade(t, gx, gy, gz, state):
    v_sum, vt_sum, vu_sum, cover = state
    opacity = 0.6 * pl.reciprocal(1.0 + jnp.exp2(jnp.minimum(13.2 * LOG2E - (6.0 * LOG2E) * t, 126.0)))
    tanh_t = jnp.tanh(t)
    tanh_u = jnp.tanh(t + 0.25)
    light = 0.48 * gx + 0.6 * gy + 0.64 * gz
    inv = lax.rsqrt(gx * gx + gy * gy + gz * gz + ONE)
    diffuse = jnp.maximum(light, 0.0) * inv
    half = jnp.maximum(light + gz, 0.0) * inv
    half = half * half
    half = half * half
    shading = 0.25 + 0.6 * diffuse + SPEC * (half * half)
    part = (1.0 - cover) * opacity
    value = part * shading
    return v_sum + value, vt_sum + value * tanh_t, vu_sum + value * tanh_u, cover + part


def render(smooth_rows, slope_rows, shape, count):
    zero = jnp.zeros(shape, jnp.float32)
    state = (zero, zero, zero, zero)
    chains = [[None] * 4 for _ in range(3)]
    for index in range(count + 4):
        a, b, c, d, e = smooth_rows(index)
        inputs = [gauss_rows(a, b, c, d, e), (e - a) + 2.0 * (d - b), gauss_rows(*slope_rows(index))]
        totals, diff = [], None
        for which, (chain, x) in enumerate(zip(chains, inputs)):
            for level in range(4):
                before, chain[level] = chain[level], x
                if before is None:
                    x = None
                    break
                if which == 0 and level == 3:
                    diff = x - before
                x = x + before
            totals.append(x)
        if index >= 4:
            state = shade(totals[0], totals[2], totals[1], diff, state)
    return state


def over(front, back):
    rest = 1.0 - front[3]
    return tuple(f + rest * b for f, b in zip(front, back))


def plane_slots(size, depth, last, info):
    planes = depth * (size // 2)
    extra = 4 if last else 0
    chip, front = info[0], info[2]
    start = 2 * front + extra * (1 - front)
    slots = [(chip ^ step) * depth + plane + start for step in range(size // 2) for plane in range(depth)]
    return slots + [(planes + 2) * front + plane for plane in range(extra)], (1 - front) * (planes + extra)


def render_kernel(size, last, info, weights, *refs):
    blocks, (image, sx, dx) = refs[:-3], refs[-3:]
    depth, own = blocks[0].shape[0], image.shape[1]
    slots, empty = plane_slots(size, depth, last, info)
    for out in (sx, dx):
        out[pl.ds(empty, 2)] = jnp.zeros((2,) + out.shape[1:], jnp.float32)
    for index, slot in enumerate(slots):
        filter_columns(blocks[index // depth], index % depth, own, weights, sx, dx, slot)

    @pl.loop(0, own // TILE)
    def _(tile):
        first = pl.multiple_of(tile * TILE, TILE)

        def rows_of(ref):
            return lambda index: [ref[index, pl.ds(first + 6 + k, TILE), :] for k in range(5)]

        total = render(rows_of(sx), rows_of(dx), (TILE, sx.shape[2]), len(slots) - 2)
        for channel in range(4):
            image[channel, pl.ds(first, TILE), :] = total[channel]


def edge_kernel(*refs):
    blocks, out = refs[:-1], refs[-1]
    own, width = blocks[0].shape[1] - 8, blocks[0].shape[2]
    places = [(block, plane) for block in blocks for plane in range(block.shape[0])]
    group = LANES // 8
    lane = lax.broadcasted_iota(jnp.int32, (own + 8, width), 1) // 8
    for base in range(0, len(places), group):
        packed = jnp.zeros((own + 8, width), jnp.float32)
        for at, (block, plane) in enumerate(places[base : base + group]):
            packed = jnp.where(lane == at, pltpu.roll(block[plane], (8 * at + 4) % width, 1), packed)
        for part, rows in enumerate((packed[0:own], packed[own:])):
            missing = LANES - rows.shape[0]
            if missing:
                rows = jnp.concatenate([rows, jnp.zeros((missing, width), jnp.float32)], 0)
            out[part, base : base + group] = jnp.transpose(rows).reshape(group, 8, LANES)


def render_edges(size, depth, last, own, info, mine, before, after, sx, dx):
    slots, empty = plane_slots(size, depth, last, info)
    count = len(slots)
    lane = lax.broadcasted_iota(jnp.int32, (count, 8, LANES), 2)
    line = lax.broadcasted_iota(jnp.int32, (count, 8, 2 * LANES), 1)

    def all_rows(ref):
        main, around = ref[0, 0:count], ref[1, 0:count]
        if own < LANES:
            main = jnp.where(lane < own, main, pltpu.roll(around, own - 2, 2))
        return jnp.concatenate([main, pltpu.roll(around, LANES - 2, 2)], 2)

    mid = all_rows(mine)
    left = jnp.where(info[3] == 1, all_rows(before), 0.0)
    right = jnp.where(info[4] == 1, all_rows(after), 0.0)
    end = jnp.where(line < 4, mid, right)
    top = jnp.where(line < 4, left, mid)
    taps = [jnp.where(line < 2, end, top)]
    for k in range(1, 5):
        taps.append(jnp.where(line < 2, pltpu.roll(end, 8 - k, 1), pltpu.roll(top, 8 - k, 1)))
    a, b, c, d, e = taps
    smooth = SCALE * gauss_rows(a, b, c, d, e)
    slope = SCALE * ((e - a) + 2.0 * (d - b))
    for out, values in ((sx, smooth), (dx, slope)):
        out[pl.ds(empty, 2)] = jnp.zeros((2,) + out.shape[1:], jnp.float32)
        for index, slot in enumerate(slots):
            out[slot] = values[index]

    def rows_of(ref):
        def five(index):
            rows = ref[index]
            return [pltpu.roll(rows, k % (2 * LANES), 1)[:, :LANES] for k in (2, 1, 0, -1, -2)]

        return five

    return render(rows_of(sx), rows_of(dx), (8, LANES), count - 2)


def with_edges(state, image):
    own, width = image.shape[1:]
    rows = jnp.concatenate(list(state) + [jnp.zeros((LANES - 32, LANES), jnp.float32)], 0)
    columns = jnp.transpose(rows)[0:own]
    lane = lax.broadcasted_iota(jnp.int32, columns.shape, 1)
    inside = (lane >= 2) & (lane < width - 2)
    return [
        jnp.where(inside, image[channel], pltpu.roll(columns, width - 2 - 8 * channel, 1)) for channel in range(4)
    ]


def fix_kernel(size, depth, info, mine, before, after, image, out, sx, dx):
    state = render_edges(size, depth, False, image.shape[1], info, mine, before, after, sx, dx)
    for channel, values in enumerate(with_edges(state, image)):
        out[channel] = values


def join_kernel(size, depth, info, mine, before, after, own_part, other, picture, sx, dx):
    state = render_edges(size, depth, True, picture.shape[1], info, mine, before, after, sx, dx)
    is_front = info[2] == 1
    mine = with_edges(state, own_part)
    other = tuple(other[channel] for channel in range(4))
    ahead = tuple(jnp.where(is_front, m, o) for m, o in zip(mine, other))
    behind = tuple(jnp.where(is_front, o, m) for m, o in zip(mine, other))
    v_sum, vt_sum, vu_sum, cover = over(ahead, behind)
    picture[0] = 0.5 * (v_sum + vu_sum)
    picture[1] = 0.5 * v_sum + 0.4 * vt_sum
    picture[2] = 0.5 * (v_sum - vt_sum)
    picture[3] = cover


def rows_around(field, plane, target, own):
    height, width = field.shape[1:]
    line = lax.broadcasted_iota(jnp.int32, (8, width), 0)
    start = target * own
    above = pl.multiple_of(jnp.maximum(start - 8, 0), 8)
    below = pl.multiple_of(jnp.minimum(start + own, height - 8), 8)
    top = jnp.where(target > 0, pltpu.roll(field[plane, pl.ds(above, 8), :], 2, 0), 0.0)
    end = jnp.where(start + own < height, pltpu.roll(field[plane, pl.ds(below, 8), :], 2, 0), 0.0)
    return jnp.where(line < 2, top, jnp.where(line < 4, end, 0.0))


def targets(size, info):
    chip, core, front = info[0], info[1], info[2]
    for chunk in range(2):
        base = front * size if chunk == 0 else (1 - front) * size
        for step in range(size // 2):
            yield chunk * (size // 2) + step, base + 2 * (chip ^ step), core


def pack_kernel(size, shared, info, source, *refs):
    outs = refs[-size:]
    depth, own = source.shape[0], outs[0].shape[1] - 8
    for index, target, core in targets(size, info):
        target = target + core
        start = pl.multiple_of(target * own, 8)
        for plane in range(depth):
            slot = (1 - core if shared else core) * depth + plane
            outs[index][slot, 0:own, :] = source[plane, pl.ds(start, own), :]
            outs[index][slot, own : own + 8, :] = rows_around(source, plane, target, own)


def pick_kernel(size, info, *refs):
    blocks, out = refs[:-1], refs[-1]
    depth = blocks[0].shape[0]
    chip, front = info[0], info[2]
    count = 4 // depth
    for part in range(count):
        wanted = chip ^ (front * (size // 2 - count) + part)
        for step in range(size // 2):

            @pl.when(wanted == step)
            def _():
                out[part * depth : (part + 1) * depth] = blocks[step][...]


SMEM = pl.BlockSpec(memory_space=pltpu.SMEM)
VMEM = pl.BlockSpec(memory_space=pltpu.VMEM)
PARAMS = pltpu.CompilerParams(vmem_limit_bytes=20 * 1024 * 1024)


def cost(flops, size):
    return pl.CostEstimate(flops=flops, bytes_accessed=size, transcendentals=0)


def local(field):
    groups = lax.axis_size("depth")
    columns = lax.axis_size("cols")
    size = groups // 2
    depth, height, width = field.shape
    own = height // groups
    me = lax.axis_index("depth")
    column = lax.axis_index("cols")
    has_left, has_right = column > 0, column < columns - 1
    info = jnp.stack([me % size // 2, me % 2, 1 - me // size, has_left, has_right]).astype(jnp.int32)
    weights = jnp.asarray(column_weights(width))
    f32 = jnp.float32
    steps = size // 2
    block = jax.ShapeDtypeStruct((2 * depth, own + 8, width), f32)
    image = jax.ShapeDtypeStruct((4, own, width), f32)

    shared = lax.ppermute(field, "depth", [(i, i ^ 1) for i in range(groups)])
    blocks = ()
    for source in (field, shared):
        blocks = pl.pallas_call(
            functools.partial(pack_kernel, size, source is shared),
            out_shape=(block,) * size,
            in_specs=[SMEM, VMEM] + [VMEM] * len(blocks),
            out_specs=(VMEM,) * size,
            input_output_aliases={2 + i: i for i in range(len(blocks))},
            compiler_params=PARAMS,
            name="pack_shared" if source is shared else "pack_own",
        )(info, source, *blocks)

    def call(kernel, name, out_shape, *args, **more):
        return pl.pallas_call(
            kernel,
            out_shape=out_shape,
            in_specs=[SMEM] + [VMEM] * (len(args) - 1),
            out_specs=jax.tree.map(lambda _: VMEM, out_shape),
            compiler_params=PARAMS,
            cost_estimate=cost(1000, 1000),
            name=name,
            **more,
        )(*args)

    def columns_near(parts):
        count = sum(part.shape[0] for part in parts)
        group = LANES // 8
        edges = pl.pallas_call(
            edge_kernel,
            out_shape=jax.ShapeDtypeStruct((2, -(-count // group) * group, 8, LANES), f32),
            in_specs=[VMEM] * len(parts),
            out_specs=VMEM,
            compiler_params=PARAMS,
            cost_estimate=cost(1000, 1000),
            name="edge_columns",
        )(*parts)
        if columns == 2:
            return (edges,) + (lax.ppermute(edges, "cols", [(0, 1), (1, 0)]),) * 2
        return (edges,) + tuple(
            lax.ppermute(edges, "cols", [(i, i + shift) for i in range(columns) if 0 <= i + shift < columns])
            for shift in (1, -1)
        )

    def plane_scratch(last, rows, lanes):
        return [pltpu.VMEM((depth * size + (6 if last else 2), rows, lanes), f32)] * 2

    def render_call(last, parts):
        kernel = functools.partial(render_kernel, size, last)
        scratch = plane_scratch(last, own + 16, width)
        name = "render_last" if last else "render_first"
        return call(kernel, name, image, info, weights, *parts, scratch_shapes=scratch)

    pick = pl.pallas_call(
        functools.partial(pick_kernel, size),
        out_shape=jax.ShapeDtypeStruct((4,) + block.shape[1:], f32),
        in_specs=[SMEM] + [VMEM] * (size // 2),
        out_specs=VMEM,
        compiler_params=PARAMS,
        cost_estimate=cost(1000, 1000),
        name="pick_boundary",
    )

    def swap(x, bits):
        return lax.ppermute(x, "depth", [(i, i ^ bits) for i in range(groups)])

    def gathered(parts):
        return [parts[0]] + [swap(parts[step], 2 * step) for step in range(1, steps)]

    theirs = gathered(blocks[:steps])
    boundary = swap(pick(info, *theirs), size)
    first_image = render_call(False, theirs)
    kernel = functools.partial(fix_kernel, size, 2 * depth)
    scratch = plane_scratch(False, 8, 2 * LANES)
    first_image = call(
        kernel, "first_edges", image, info, *columns_near(theirs), first_image, scratch_shapes=scratch
    )
    image_part = swap(first_image, size)
    mine = [blocks[steps]]
    for step in range(1, steps):
        held, _ = lax.optimization_barrier((blocks[steps + step], theirs[step]))
        mine.append(swap(held, 2 * step))
    parts, _ = lax.optimization_barrier((mine + [boundary], first_image))
    own_part = render_call(True, parts)
    kernel = functools.partial(join_kernel, size, 2 * depth)
    scratch = plane_scratch(True, 8, 2 * LANES)
    return call(
        kernel, "join_halves", image, info, *columns_near(parts), own_part, image_part, scratch_shapes=scratch
    )


def solution(mesh):
    return jax.shard_map(
        local,
        mesh=mesh,
        in_specs=(P("depth", None, "cols"),),
        out_specs=P(None, "depth", "cols"),
        check_vma=False,
    )
```

```python
import functools
import math

import jax
import jax.numpy as jnp
import numpy as np
from jax import lax
from jax.experimental import pallas as pl
from jax.experimental.pallas import tpu as pltpu
from jax.sharding import PartitionSpec as P

GAUSS = (1.0, 4.0, 6.0, 4.0, 1.0)
DERIV = (-1.0, -2.0, 0.0, 2.0, 1.0)
SCALE = 7.0 / 4096.0
ONE = 49.0 / 256.0
HALF_LEN = math.sqrt(0.48 * 0.48 + 0.6 * 0.6 + 1.64 * 1.64)
SPEC = 0.35 / HALF_LEN**8
LANES = 128
TILE = 16


def column_weights(width):
    body = np.zeros((width, 2 * width), np.float32)
    for out in range(width):
        for k in range(5):
            if 0 <= out - 2 + k < width:
                body[out - 2 + k, out] = SCALE * GAUSS[k]
                body[out - 2 + k, width + out] = SCALE * DERIV[k]
    return np.concatenate([body, body, body], 0).astype(jnp.bfloat16)


def three_parts(x):
    hi = x.astype(jnp.bfloat16)
    rest = x - hi.astype(jnp.float32)
    mid = rest.astype(jnp.bfloat16)
    lo = (rest - mid.astype(jnp.float32)).astype(jnp.bfloat16)
    return hi, mid, lo


def filter_columns(planes, index, weights, sx, dx):
    width = planes.shape[2]
    row = jnp.concatenate(three_parts(planes[index]), 1)
    both = jnp.dot(row, weights[...], preferred_element_type=jnp.float32)
    sx[index] = both[:, :width]
    dx[index] = both[:, width:]


def gauss_rows(a, b, c, d, e):
    return (a + e) + 4.0 * (b + d) + 6.0 * c


def shade(t, gx, gy, gz, state):
    v_sum, vt_sum, vu_sum, cover = state
    opacity = pl.reciprocal(1.0 / 0.6 + jnp.exp(jnp.minimum((13.2 - math.log(0.6)) - 6.0 * t, 80.0)))
    tanh_t = jnp.tanh(t)
    tanh_u = jnp.tanh(t + 0.25)
    light = 0.48 * gx + 0.6 * gy + 0.64 * gz
    inv = lax.rsqrt(gx * gx + gy * gy + gz * gz + ONE)
    diffuse = jnp.maximum(light, 0.0) * inv
    half = jnp.maximum(light + gz, 0.0) * inv
    half = half * half
    half = half * half
    shading = 0.25 + 0.6 * diffuse + SPEC * (half * half)
    part = (1.0 - cover) * opacity
    value = part * shading
    return v_sum + value, vt_sum + value * tanh_t, vu_sum + value * tanh_u, cover + part


def render(smooth_rows, slope_rows, shape, count):
    zero = jnp.zeros(shape, jnp.float32)
    state = (zero, zero, zero, zero)
    chains = [[None] * 4 for _ in range(3)]
    for index in range(count + 4):
        a, b, c, d, e = smooth_rows(index)
        inputs = [gauss_rows(a, b, c, d, e), (e - a) + 2.0 * (d - b), gauss_rows(*slope_rows(index))]
        totals, diff = [], None
        for which, (chain, x) in enumerate(zip(chains, inputs)):
            for level in range(4):
                before, chain[level] = chain[level], x
                if before is None:
                    x = None
                    break
                if which == 0 and level == 3:
                    diff = x - before
                x = x + before
            totals.append(x)
        if index >= 4:
            state = shade(totals[0], totals[2], totals[1], diff, state)
    return state


def over(front, back):
    rest = 1.0 - front[3]
    return tuple(f + rest * b for f, b in zip(front, back))


def plane_slots(size, depth, last, info):
    planes = depth * (size // 2)
    extra = 4 if last else 0
    chip, front = info[0], info[2]
    start = 2 * front + extra * (1 - front)
    slots = [(chip ^ step) * depth + plane + start for step in range(size // 2) for plane in range(depth)]
    return slots + [(planes + 2) * front + plane for plane in range(extra)], (1 - front) * (planes + extra)


def render_kernel(size, depth, last, info, weights, *refs):
    blocks, (image, planes, cubed, sx, dx) = refs[:-5], refs[-5:]
    own, width = image.shape[1:]
    slots, empty = plane_slots(size, depth, last, info)
    planes[pl.ds(empty, 2)] = jnp.zeros((2,) + planes.shape[1:], jnp.float32)
    places = [(block, plane) for block in blocks for plane in range(block.shape[0])]
    for (block, plane), slot in zip(places, slots):
        planes[slot, 8 : 8 + own] = block[plane, 0:own]
        planes[slot, 6:8] = block[plane, own : own + 2]
        planes[slot, 8 + own : 10 + own] = block[plane, own + 2 : own + 4]

    def cube(first, rows):
        chain = [None] * 3
        for index in range(planes.shape[0]):
            a, b, c, d = (planes[index, pl.ds(first + 6 + k, rows), :] for k in range(4))
            x = (a + d) + 3.0 * (b + c)
            for level in range(3):
                before, chain[level] = chain[level], x
                if before is None:
                    x = None
                    break
                x = x + before
            if x is not None:
                cubed[index - 3, pl.ds(first, rows), :] = x

    @pl.loop(0, own // TILE)
    def _(tile):
        cube(pl.multiple_of(tile * TILE, TILE), TILE)

    cube(own, 8)
    for index in range(cubed.shape[0]):
        filter_columns(cubed, index, weights, sx, dx)

    @pl.loop(0, own // TILE)
    def _(tile):
        first = pl.multiple_of(tile * TILE, TILE)
        zero = jnp.zeros((TILE, width), jnp.float32)
        state = (zero, zero, zero, zero)
        for index in range(cubed.shape[0]):
            a, b, c, d = (ref[index, pl.ds(first + k, TILE), :] for ref in (sx, dx) for k in range(2))
            now = (a + b, b - a, c + d)
            if index:
                t, gy, gx = (x + y for x, y in zip(before, now))
                state = shade(t, gx, gy, now[0] - before[0], state)
            before = now
        for channel in range(4):
            image[channel, pl.ds(first, TILE), :] = state[channel]


def edge_kernel(*refs):
    blocks, (out, sent) = refs[:-2], refs[-2:]
    own, width = blocks[0].shape[1] - 8, blocks[0].shape[2]
    places = [(block, plane) for block in blocks for plane in range(block.shape[0])]
    group = LANES // 8
    lane = lax.broadcasted_iota(jnp.int32, (own + 8, width), 1) // 8
    for base in range(0, len(places), group):
        packed = jnp.zeros((own + 8, width), jnp.float32)
        for at, (block, plane) in enumerate(places[base : base + group]):
            packed = jnp.where(lane == at, pltpu.roll(block[plane], (8 * at + 4) % width, 1), packed)
        for part, rows in enumerate((packed[0:own], packed[own:])):
            missing = LANES - rows.shape[0]
            if missing:
                rows = jnp.concatenate([rows, jnp.zeros((missing, width), jnp.float32)], 0)
            out[part, base : base + group] = jnp.transpose(rows).reshape(group, 8, LANES)
    line = lax.broadcasted_iota(jnp.int32, (8, LANES), 0)
    pairs = -(-len(places) // 2)
    for pair in range(pairs):
        sent[pair] = jnp.where(line < 4, pltpu.roll(out[0, 2 * pair], 6, 0), pltpu.roll(out[0, 2 * pair + 1], 2, 0))
    lane = lax.broadcasted_iota(jnp.int32, (8, LANES), 1) // 4
    for base in range(0, len(places), LANES // 4):
        packed = jnp.zeros((8, LANES), jnp.float32)
        for at in range(min(LANES // 4, len(places) - base)):
            packed = jnp.where(lane == at, pltpu.roll(out[1, base + at], 4 * at, 1), packed)
        sent[pairs + base // (LANES // 4)] = packed


def sent_tiles(count):
    return -(-count // 2) + -(-count // (LANES // 4))


def received_edges(sent, count):
    pairs = -(-count // 2)
    own = jnp.stack([pltpu.roll(sent[0:pairs], 2, 1), pltpu.roll(sent[0:pairs], 6, 1)], 1)
    own = own.reshape(2 * pairs, 8, LANES)[0:count]
    group = LANES // 4
    turns = [(LANES - 4 * (index % group)) % LANES for index in range(count)]
    around = [pltpu.roll(sent[pairs + index // group], turn, 1) for index, turn in enumerate(turns)]
    return own, jnp.stack(around, 0)


def render_edges(size, depth, last, own, info, mine, before, after, sx, dx):
    slots, empty = plane_slots(size, depth, last, info)
    count = len(slots)
    lane = lax.broadcasted_iota(jnp.int32, (count, 8, LANES), 2)
    line = lax.broadcasted_iota(jnp.int32, (count, 8, 2 * LANES), 1)

    def all_rows(main, around):
        if own < LANES:
            main = jnp.where(lane < own, main, pltpu.roll(around, own - 2, 2))
        return jnp.concatenate([main, pltpu.roll(around, LANES - 2, 2)], 2)

    mid = all_rows(mine[0, 0:count], mine[1, 0:count])
    if before is after:
        left = right = all_rows(*received_edges(before, count))
    else:
        left, right = all_rows(*received_edges(before, count)), all_rows(*received_edges(after, count))
    left = jnp.where(info[3] == 1, left, 0.0)
    right = jnp.where(info[4] == 1, right, 0.0)
    end = jnp.where(line < 4, mid, right)
    top = jnp.where(line < 4, left, mid)
    taps = [jnp.where(line < 2, end, top)]
    for k in range(1, 5):
        taps.append(jnp.where(line < 2, pltpu.roll(end, 8 - k, 1), pltpu.roll(top, 8 - k, 1)))
    a, b, c, d, e = taps
    smooth = SCALE * gauss_rows(a, b, c, d, e)
    slope = SCALE * ((e - a) + 2.0 * (d - b))
    for out, values in ((sx, smooth), (dx, slope)):
        out[pl.ds(empty, 2)] = jnp.zeros((2,) + out.shape[1:], jnp.float32)
        for index, slot in enumerate(slots):
            out[slot] = values[index]

    def rows_of(ref):
        def five(index):
            rows = ref[index]
            return [pltpu.roll(rows, k % (2 * LANES), 1)[:, :LANES] for k in (2, 1, 0, -1, -2)]

        return five

    return render(rows_of(sx), rows_of(dx), (8, LANES), count - 2)


def with_edges(state, image):
    own, width = image.shape[1:]
    rows = jnp.concatenate(list(state) + [jnp.zeros((LANES - 32, LANES), jnp.float32)], 0)
    columns = jnp.transpose(rows)[0:own]
    lane = lax.broadcasted_iota(jnp.int32, columns.shape, 1)
    inside = (lane >= 2) & (lane < width - 2)
    return [
        jnp.where(inside, image[channel], pltpu.roll(columns, width - 2 - 8 * channel, 1)) for channel in range(4)
    ]


def fix_kernel(size, depth, info, image, mine, *refs):
    before, after, (out, sx, dx) = refs[0], refs[-4], refs[-3:]
    state = render_edges(size, depth, False, image.shape[1], info, mine, before, after, sx, dx)
    for channel, values in enumerate(with_edges(state, image)):
        out[channel] = values


def join_kernel(size, depth, info, image, other, mine, *refs):
    before, after, (picture, sx, dx) = refs[0], refs[-4], refs[-3:]
    state = render_edges(size, depth, True, image.shape[1], info, mine, before, after, sx, dx)
    mine = with_edges(state, image)
    is_front = info[2] == 1
    other = tuple(other[channel] for channel in range(4))
    ahead = tuple(jnp.where(is_front, m, o) for m, o in zip(mine, other))
    behind = tuple(jnp.where(is_front, o, m) for m, o in zip(mine, other))
    v_sum, vt_sum, vu_sum, cover = over(ahead, behind)
    picture[0] = 0.5 * (v_sum + vu_sum)
    picture[1] = 0.5 * v_sum + 0.4 * vt_sum
    picture[2] = 0.5 * (v_sum - vt_sum)
    picture[3] = cover


def rows_around(field, plane, target, own):
    height, width = field.shape[1:]
    line = lax.broadcasted_iota(jnp.int32, (8, width), 0)
    start = target * own
    above = pl.multiple_of(jnp.maximum(start - 8, 0), 8)
    below = pl.multiple_of(jnp.minimum(start + own, height - 8), 8)
    top = jnp.where(target > 0, pltpu.roll(field[plane, pl.ds(above, 8), :], 2, 0), 0.0)
    end = jnp.where(start + own < height, pltpu.roll(field[plane, pl.ds(below, 8), :], 2, 0), 0.0)
    return jnp.where(line < 2, top, jnp.where(line < 4, end, 0.0))


def targets(size, info):
    chip, core, front = info[0], info[1], info[2]
    for chunk in range(2):
        base = front * size if chunk == 0 else (1 - front) * size
        for step in range(size // 2):
            yield chunk * (size // 2) + step, base + 2 * (chip ^ step), core


def pack_kernel(size, shared, info, source, *refs):
    outs = refs[-size:]
    depth, own = source.shape[0], outs[0].shape[1] - 8
    for index, target, core in targets(size, info):
        target = target + core
        start = pl.multiple_of(target * own, 8)
        for plane in range(depth):
            slot = (1 - core if shared else core) * depth + plane
            outs[index][slot, 0:own, :] = source[plane, pl.ds(start, own), :]
            outs[index][slot, own : own + 8, :] = rows_around(source, plane, target, own)


def pick_kernel(size, info, *refs):
    blocks, out = refs[:-1], refs[-1]
    depth = blocks[0].shape[0]
    chip, front = info[0], info[2]
    count = 4 // depth
    for part in range(count):
        wanted = chip ^ (front * (size // 2 - count) + part)
        for step in range(size // 2):

            @pl.when(wanted == step)
            def _():
                out[part * depth : (part + 1) * depth] = blocks[step][...]


SMEM = pl.BlockSpec(memory_space=pltpu.SMEM)
VMEM = pl.BlockSpec(memory_space=pltpu.VMEM)
PARAMS = pltpu.CompilerParams(vmem_limit_bytes=20 * 1024 * 1024)


def cost(flops, size):
    return pl.CostEstimate(flops=flops, bytes_accessed=size, transcendentals=0)


def local(field):
    groups = lax.axis_size("depth")
    columns = lax.axis_size("cols")
    size = groups // 2
    depth, height, width = field.shape
    own = height // groups
    me = lax.axis_index("depth")
    column = lax.axis_index("cols")
    has_left, has_right = column > 0, column < columns - 1
    info = jnp.stack([me % size // 2, me % 2, 1 - me // size, has_left, has_right]).astype(jnp.int32)
    weights = jnp.asarray(column_weights(width))
    f32 = jnp.float32
    steps = size // 2
    block = jax.ShapeDtypeStruct((2 * depth, own + 8, width), f32)
    image = jax.ShapeDtypeStruct((4, own, width), f32)

    shared = lax.ppermute(field, "depth", [(i, i ^ 1) for i in range(groups)])
    blocks = ()
    for source in (field, shared):
        blocks = pl.pallas_call(
            functools.partial(pack_kernel, size, source is shared),
            out_shape=(block,) * size,
            in_specs=[SMEM, VMEM] + [VMEM] * len(blocks),
            out_specs=(VMEM,) * size,
            input_output_aliases={2 + i: i for i in range(len(blocks))},
            compiler_params=PARAMS,
            name="pack_shared" if source is shared else "pack_own",
        )(info, source, *blocks)

    def call(kernel, name, out_shape, *args, **more):
        return pl.pallas_call(
            kernel,
            out_shape=out_shape,
            in_specs=[SMEM] + [VMEM] * (len(args) - 1),
            out_specs=jax.tree.map(lambda _: VMEM, out_shape),
            compiler_params=PARAMS,
            cost_estimate=cost(1000, 1000),
            name=name,
            **more,
        )(*args)

    def columns_near(parts):
        count = sum(part.shape[0] for part in parts)
        group = LANES // 8
        edges, sent = pl.pallas_call(
            edge_kernel,
            out_shape=(
                jax.ShapeDtypeStruct((2, -(-count // group) * group, 8, LANES), f32),
                jax.ShapeDtypeStruct((sent_tiles(count), 8, LANES), f32),
            ),
            in_specs=[VMEM] * len(parts),
            out_specs=(VMEM, VMEM),
            compiler_params=PARAMS,
            cost_estimate=cost(1000, 1000),
            name="edge_columns",
        )(*parts)
        if columns == 2:
            return edges, lax.ppermute(sent, "cols", [(0, 1), (1, 0)])
        return (edges,) + tuple(
            lax.ppermute(sent, "cols", [(i, i + shift) for i in range(columns) if 0 <= i + shift < columns])
            for shift in (1, -1)
        )

    def render_call(last, parts):
        count = depth * size + (6 if last else 2)
        scratch = [pltpu.VMEM((count, own + 24, width), f32)] + [pltpu.VMEM((count - 3, own + 8, width), f32)] * 3
        kernel = functools.partial(render_kernel, size, 2 * depth, last)
        name = "render_last" if last else "render_first"
        return call(kernel, name, image, info, weights, *parts, scratch_shapes=scratch)

    def edge_scratch(last):
        return [pltpu.VMEM((depth * size + (6 if last else 2), 8, 2 * LANES), f32)] * 2

    pick = pl.pallas_call(
        functools.partial(pick_kernel, size),
        out_shape=jax.ShapeDtypeStruct((4,) + block.shape[1:], f32),
        in_specs=[SMEM] + [VMEM] * (size // 2),
        out_specs=VMEM,
        compiler_params=PARAMS,
        cost_estimate=cost(1000, 1000),
        name="pick_boundary",
    )

    def swap(x, bits):
        return lax.ppermute(x, "depth", [(i, i ^ bits) for i in range(groups)])

    def gathered(parts):
        return [parts[0]] + [swap(parts[step], 2 * step) for step in range(1, steps)]

    theirs = gathered(blocks[:steps])
    boundary = swap(pick(info, *theirs), size)
    first_image = render_call(False, theirs)
    kernel = functools.partial(fix_kernel, size, 2 * depth)
    near = columns_near(theirs)
    first_image = call(kernel, "first_edges", image, info, first_image, *near, scratch_shapes=edge_scratch(False))
    image_part = swap(first_image, size)
    mine = [blocks[steps]]
    for step in range(1, steps):
        held, _ = lax.optimization_barrier((blocks[steps + step], theirs[step]))
        mine.append(swap(held, 2 * step))
    parts, _ = lax.optimization_barrier((mine + [boundary], first_image))
    own_part = render_call(True, parts)
    kernel = functools.partial(join_kernel, size, 2 * depth)
    near = columns_near(parts)
    return call(kernel, "join_halves", image, info, own_part, image_part, *near, scratch_shapes=edge_scratch(True))


def solution(mesh):
    return jax.shard_map(
        local,
        mesh=mesh,
        in_specs=(P("depth", None, "cols"),),
        out_specs=P(None, "depth", "cols"),
        check_vma=False,
    )
```

```python
import functools
import math

import jax
import jax.numpy as jnp
import numpy as np
from jax import lax
from jax.experimental import pallas as pl
from jax.experimental.pallas import tpu as pltpu
from jax.sharding import PartitionSpec as P

GAUSS = (1.0, 4.0, 6.0, 4.0, 1.0)
DERIV = (-1.0, -2.0, 0.0, 2.0, 1.0)
SCALE = 7.0 / 4096.0
ONE = 49.0 / 256.0
HALF_LEN = math.sqrt(0.48 * 0.48 + 0.6 * 0.6 + 1.64 * 1.64)
SPEC = 0.35 / HALF_LEN**8
LANES = 128
TILE = 16


def column_weights(width):
    body = np.zeros((width, 2 * width), np.float32)
    for out in range(width):
        for k in range(5):
            if 0 <= out - 2 + k < width:
                body[out - 2 + k, out] = SCALE * GAUSS[k]
                body[out - 2 + k, width + out] = SCALE * DERIV[k]
    return np.concatenate([body, body, body], 0).astype(jnp.bfloat16)


def three_parts(x):
    hi = x.astype(jnp.bfloat16)
    rest = x - hi.astype(jnp.float32)
    mid = rest.astype(jnp.bfloat16)
    lo = (rest - mid.astype(jnp.float32)).astype(jnp.bfloat16)
    return hi, mid, lo


def filter_columns(planes, index, weights, sx, dx):
    width = planes.shape[2]
    row = jnp.concatenate(three_parts(planes[index]), 1)
    both = jnp.dot(row, weights[...], preferred_element_type=jnp.float32)
    sx[index] = both[:, :width]
    dx[index] = both[:, width:]


def gauss_rows(a, b, c, d, e):
    return (a + e) + 4.0 * (b + d) + 6.0 * c


def shade(t, gx, gy, gz, state):
    v_sum, vt_sum, vu_sum, cover = state
    opacity = pl.reciprocal(1.0 / 0.6 + jnp.exp(jnp.minimum((13.2 - math.log(0.6)) - 6.0 * t, 80.0)))
    tanh_t = jnp.tanh(t)
    tanh_u = jnp.tanh(t + 0.25)
    light = 0.48 * gx + 0.6 * gy + 0.64 * gz
    inv = lax.rsqrt(gx * gx + gy * gy + gz * gz + ONE)
    diffuse = jnp.maximum(light, 0.0) * inv
    half = jnp.maximum(light + gz, 0.0) * inv
    half = half * half
    half = half * half
    shading = 0.25 + 0.6 * diffuse + SPEC * (half * half)
    part = (1.0 - cover) * opacity
    value = part * shading
    return v_sum + value, vt_sum + value * tanh_t, vu_sum + value * tanh_u, cover + part


def render(smooth_rows, slope_rows, shape, count):
    zero = jnp.zeros(shape, jnp.float32)
    state = (zero, zero, zero, zero)
    chains = [[None] * 4 for _ in range(3)]
    for index in range(count + 4):
        a, b, c, d, e = smooth_rows(index)
        inputs = [gauss_rows(a, b, c, d, e), (e - a) + 2.0 * (d - b), gauss_rows(*slope_rows(index))]
        totals, diff = [], None
        for which, (chain, x) in enumerate(zip(chains, inputs)):
            for level in range(4):
                before, chain[level] = chain[level], x
                if before is None:
                    x = None
                    break
                if which == 0 and level == 3:
                    diff = x - before
                x = x + before
            totals.append(x)
        if index >= 4:
            state = shade(totals[0], totals[2], totals[1], diff, state)
    return state


def over(front, back):
    rest = 1.0 - front[3]
    return tuple(f + rest * b for f, b in zip(front, back))


def plane_slots(size, depth, last, info):
    planes = depth * (size // 2)
    extra = 4 if last else 0
    chip, front = info[0], info[2]
    start = 2 * front + extra * (1 - front)
    slots = [(chip ^ step) * depth + plane + start for step in range(size // 2) for plane in range(depth)]
    return slots + [(planes + 2) * front + plane for plane in range(extra)], (1 - front) * (planes + extra)


def render_kernel(size, depth, last, info, weights, *refs):
    blocks, (image, planes, cubed, sx, dx) = refs[:-5], refs[-5:]
    own, width = image.shape[1:]
    slots, empty = plane_slots(size, depth, last, info)
    planes[pl.ds(empty, 2)] = jnp.zeros((2,) + planes.shape[1:], jnp.float32)
    places = [(block, plane) for block in blocks for plane in range(depth)]
    for (block, plane), slot in zip(places, slots):
        around = depth * own + 4 * plane
        planes[slot, 8 : 8 + own] = block[plane * own : (plane + 1) * own]
        planes[slot, 6:8] = block[around : around + 2]
        planes[slot, 8 + own : 10 + own] = block[around + 2 : around + 4]

    def cube(first, rows):
        chain = [None] * 3
        for index in range(planes.shape[0]):
            a, b, c, d = (planes[index, pl.ds(first + 6 + k, rows), :] for k in range(4))
            x = (a + d) + 3.0 * (b + c)
            for level in range(3):
                before, chain[level] = chain[level], x
                if before is None:
                    x = None
                    break
                x = x + before
            if x is not None:
                cubed[index - 3, pl.ds(first, rows), :] = x

    @pl.loop(0, own // TILE)
    def _(tile):
        cube(pl.multiple_of(tile * TILE, TILE), TILE)

    cube(own, 8)
    for index in range(cubed.shape[0]):
        filter_columns(cubed, index, weights, sx, dx)

    @pl.loop(0, own // TILE)
    def _(tile):
        first = pl.multiple_of(tile * TILE, TILE)
        zero = jnp.zeros((TILE, width), jnp.float32)
        state = (zero, zero, zero, zero)
        for index in range(cubed.shape[0]):
            a, b, c, d = (ref[index, pl.ds(first + k, TILE), :] for ref in (sx, dx) for k in range(2))
            now = (a + b, b - a, c + d)
            if index:
                t, gy, gx = (x + y for x, y in zip(before, now))
                state = shade(t, gx, gy, now[0] - before[0], state)
            before = now
        for channel in range(4):
            image[channel, pl.ds(first, TILE), :] = state[channel]


def edge_columns(blocks, depth, own, out):
    width = blocks[0].shape[1]
    places = [(block, plane) for block in blocks for plane in range(depth)]
    group = LANES // 8
    for base in range(0, len(places), group):
        for part, count in enumerate((own, 4)):
            lane = lax.broadcasted_iota(jnp.int32, (count, width), 1) // 8
            packed = jnp.zeros((count, width), jnp.float32)
            for at, (block, plane) in enumerate(places[base : base + group]):
                first = part * depth * own + plane * count
                turned = pltpu.roll(block[first : first + count], (8 * at + 4) % width, 1)
                packed = jnp.where(lane == at, turned, packed)
            if count < LANES:
                packed = jnp.concatenate([packed, jnp.zeros((LANES - count, width), jnp.float32)], 0)
            out[part, base : base + group] = jnp.transpose(packed).reshape(group, 8, LANES)


def sent_tiles(count):
    return -(-count // 2) + -(-count // (LANES // 4))


def edge_kernel(depth, own, *refs):
    blocks, (out, sent) = refs[:-2], refs[-2:]
    edge_columns(blocks, depth, own, out)
    count = depth * len(blocks)
    line = lax.broadcasted_iota(jnp.int32, (8, LANES), 0)
    pairs = -(-count // 2)
    for pair in range(pairs):
        sent[pair] = jnp.where(line < 4, pltpu.roll(out[0, 2 * pair], 6, 0), pltpu.roll(out[0, 2 * pair + 1], 2, 0))
    lane = lax.broadcasted_iota(jnp.int32, (8, LANES), 1) // 4
    for base in range(0, count, LANES // 4):
        packed = jnp.zeros((8, LANES), jnp.float32)
        for at in range(min(LANES // 4, count - base)):
            packed = jnp.where(lane == at, pltpu.roll(out[1, base + at], 4 * at, 1), packed)
        sent[pairs + base // (LANES // 4)] = packed


def near_tiles(info, count, before, after, near):
    pairs = -(-count // 2)
    left = jnp.where(info[3] == 1, before[...], 0.0)
    right = jnp.where(info[4] == 1, after[...], 0.0)
    line = lax.broadcasted_iota(jnp.int32, left.shape, 1)
    near[0:pairs] = jnp.where(line % 4 < 2, left, right)[0:pairs]
    near[pairs:] = jnp.where(line < 4, left, right)[pairs:]


def block_near(near, depth, blocks, block):
    pairs, group = depth // 2, LANES // (4 * depth)
    turn = LANES - block % group * (4 * depth)
    around = pltpu.roll(near[blocks * pairs + block // group], turn % LANES, 1)
    return [near[block * pairs + pair] for pair in range(pairs)] + [around]


def near_kernel(depth, info, before, after, *refs):
    blocks, near = refs[(len(refs) - 1) // 2 : -1], refs[-1]
    near_tiles(info, depth * len(blocks), before, after, near)
    for index, out in enumerate(blocks):
        tiles = block_near(near, depth, len(blocks), index)
        first = out.shape[0] - 8 * len(tiles)
        for at, tile in enumerate(tiles):
            out[first + 8 * at : first + 8 * at + 8] = tile


def neighbour_columns(depth, tiles):
    own, around = [], []
    for block in tiles:
        for plane in range(depth):
            own.append(pltpu.roll(block[plane // 2], 6 if plane % 2 else 2, 0))
            around.append(pltpu.roll(block[-1], (LANES - 4 * plane) % LANES, 1))
    return jnp.stack(own, 0), jnp.stack(around, 0)


def filter_edges(own, mine, tiles, depth, slots, sx, dx):
    count = len(slots)
    lane = lax.broadcasted_iota(jnp.int32, (count, 8, LANES), 2)
    line = lax.broadcasted_iota(jnp.int32, (count, 8, 2 * LANES), 1)

    def all_rows(main, around):
        if own < LANES:
            main = jnp.where(lane < own, main, pltpu.roll(around, own - 2, 2))
        return jnp.concatenate([main, pltpu.roll(around, LANES - 2, 2)], 2)

    mid = all_rows(mine[0, 0:count], mine[1, 0:count])
    beside = all_rows(*neighbour_columns(depth, tiles))
    end = jnp.where(line < 4, mid, beside)
    top = jnp.where(line < 4, beside, mid)
    taps = [jnp.where(line < 2, end, top)]
    for k in range(1, 5):
        taps.append(jnp.where(line < 2, pltpu.roll(end, 8 - k, 1), pltpu.roll(top, 8 - k, 1)))
    a, b, c, d, e = taps
    smooth = SCALE * gauss_rows(a, b, c, d, e)
    slope = SCALE * ((e - a) + 2.0 * (d - b))
    for index, slot in enumerate(slots):
        sx[slot] = smooth[index]
        dx[slot] = slope[index]


def clear_planes(empty, *planes):
    for out in planes:
        out[pl.ds(empty, 2)] = jnp.zeros((2,) + out.shape[1:], jnp.float32)


def render_edges(sx, dx):
    def rows_of(ref):
        def five(index):
            rows = ref[index]
            return [pltpu.roll(rows, k % (2 * LANES), 1)[:, :LANES] for k in (2, 1, 0, -1, -2)]

        return five

    return render(rows_of(sx), rows_of(dx), (8, LANES), sx.shape[0] - 4)


def with_edges(state, image):
    own, width = image.shape[1:]
    rows = jnp.concatenate(list(state) + [jnp.zeros((LANES - 32, LANES), jnp.float32)], 0)
    columns = jnp.transpose(rows)[0:own]
    lane = lax.broadcasted_iota(jnp.int32, columns.shape, 1)
    inside = (lane >= 2) & (lane < width - 2)
    return [
        jnp.where(inside, image[channel], pltpu.roll(columns, width - 2 - 8 * channel, 1)) for channel in range(4)
    ]


def fix_kernel(size, depth, info, image, mine, before, after, out, sx, dx, near):
    steps, own = size // 2, image.shape[1]
    near_tiles(info, depth * steps, before, after, near)
    tiles = [block_near(near, depth, steps, step) for step in range(steps)]
    slots, empty = plane_slots(size, depth, False, info)
    clear_planes(empty, sx, dx)
    filter_edges(own, mine, tiles, depth, slots, sx, dx)
    state = render_edges(sx, dx)
    for channel, values in enumerate(with_edges(state, image)):
        out[channel * own : (channel + 1) * own] = values
    wanted = info[0] ^ (info[2] * (steps - 1))
    for step in range(steps):

        @pl.when(wanted == step)
        def _():
            for at, tile in enumerate(tiles[step]):
                out[4 * own + 8 * at : 4 * own + 8 * at + 8] = tile


def block_tiles(source, depth):
    first = source.shape[0] - 8 * (depth // 2 + 1)
    return [source[first + 8 * at : first + 8 * at + 8] for at in range(depth // 2 + 1)]


def own_edges_kernel(size, depth, own, info, *refs):
    blocks, (sx, dx, mine) = refs[:-3], refs[-3:]
    edge_columns(blocks, depth, own, mine)
    slots, empty = plane_slots(size, depth, True, info)
    clear_planes(empty, sx, dx)
    tiles = [block_tiles(block, depth) for block in blocks]
    filter_edges(own, mine, tiles, depth, slots[:-4], sx, dx)


def join_kernel(size, depth, info, image, other, boundary, sx_own, dx_own, picture, sx, dx, mine):
    own = image.shape[1]
    edge_columns([boundary], depth, own, mine)
    filter_edges(own, mine, [block_tiles(other, depth)], depth, plane_slots(size, depth, True, info)[0][-4:], sx, dx)
    mine = with_edges(render_edges(sx, dx), image)
    is_front = info[2] == 1
    other = tuple(other[channel * own : (channel + 1) * own] for channel in range(4))
    ahead = tuple(jnp.where(is_front, m, o) for m, o in zip(mine, other))
    behind = tuple(jnp.where(is_front, o, m) for m, o in zip(mine, other))
    v_sum, vt_sum, vu_sum, cover = over(ahead, behind)
    picture[0] = 0.5 * (v_sum + vu_sum)
    picture[1] = 0.5 * v_sum + 0.4 * vt_sum
    picture[2] = 0.5 * (v_sum - vt_sum)
    picture[3] = cover


def rows_around(field, plane, target, own):
    height, width = field.shape[1:]
    line = lax.broadcasted_iota(jnp.int32, (8, width), 0)
    start = target * own
    above = pl.multiple_of(jnp.maximum(start - 8, 0), 8)
    below = pl.multiple_of(jnp.minimum(start + own, height - 8), 8)
    top = jnp.where(target > 0, pltpu.roll(field[plane, pl.ds(above, 8), :], 2, 0), 0.0)
    end = jnp.where(start + own < height, pltpu.roll(field[plane, pl.ds(below, 8), :], 2, 0), 0.0)
    return jnp.where(line < 2, top, jnp.where(line < 4, end, 0.0))


def targets(size, info):
    chip, core, front = info[0], info[1], info[2]
    for chunk in range(2):
        base = front * size if chunk == 0 else (1 - front) * size
        for step in range(size // 2):
            yield chunk * (size // 2) + step, base + 2 * (chip ^ step), core


def pack_kernel(size, own, shared, info, source, *refs):
    outs = refs[-size:]
    depth, width = source.shape[0], source.shape[2]
    line = lax.broadcasted_iota(jnp.int32, (8, width), 0)
    for index, target, core in targets(size, info):
        out, target, place = outs[index], target + core, 1 - core if shared else core
        start = pl.multiple_of(target * own, 8)
        for plane in range(depth):
            to = pl.multiple_of((place * depth + plane) * own, 8)
            out[pl.ds(to, own), :] = source[plane, pl.ds(start, own), :]
        for plane in range(0, depth, 2):
            first, second = (rows_around(source, plane + k, target, own) for k in range(2))
            to = pl.multiple_of(2 * depth * own + 4 * (place * depth + plane), 8)
            out[pl.ds(to, 8), :] = jnp.where(line < 4, first, pltpu.roll(second, 4, 0))


def pick_kernel(size, info, *refs):
    blocks, out = refs[:-1], refs[-1]
    wanted = info[0] ^ (info[2] * (size // 2 - 1))
    for step, block in enumerate(blocks):

        @pl.when(wanted == step)
        def _():
            out[...] = block[...]


SMEM = pl.BlockSpec(memory_space=pltpu.SMEM)
VMEM = pl.BlockSpec(memory_space=pltpu.VMEM)
PARAMS = pltpu.CompilerParams(vmem_limit_bytes=20 * 1024 * 1024)


def cost(flops, size):
    return pl.CostEstimate(flops=flops, bytes_accessed=size, transcendentals=0)


def local(field):
    groups = lax.axis_size("depth")
    columns = lax.axis_size("cols")
    size = groups // 2
    depth, height, width = field.shape
    own = height // groups
    me = lax.axis_index("depth")
    column = lax.axis_index("cols")
    has_left, has_right = column > 0, column < columns - 1
    info = jnp.stack([me % size // 2, me % 2, 1 - me // size, has_left, has_right]).astype(jnp.int32)
    weights = jnp.asarray(column_weights(width))
    f32 = jnp.float32
    steps = size // 2
    chip_depth = 2 * depth
    near_rows = 8 * (chip_depth // 2 + 1)
    block = wide_block = jax.ShapeDtypeStruct((chip_depth * (own + 4) + near_rows, width), f32)
    image = jax.ShapeDtypeStruct((4, own, width), f32)

    shared = lax.ppermute(field, "depth", [(i, i ^ 1) for i in range(groups)])
    blocks = ()
    for source in (field, shared):
        blocks = pl.pallas_call(
            functools.partial(pack_kernel, size, own, source is shared),
            out_shape=(block,) * steps + (wide_block,) * steps,
            in_specs=[SMEM, VMEM] + [VMEM] * len(blocks),
            out_specs=(VMEM,) * size,
            input_output_aliases={2 + i: i for i in range(len(blocks))},
            compiler_params=PARAMS,
            name="pack_shared" if source is shared else "pack_own",
        )(info, source, *blocks)

    def call(kernel, name, out_shape, *args, **more):
        return pl.pallas_call(
            kernel,
            out_shape=out_shape,
            in_specs=[SMEM] + [VMEM] * (len(args) - 1),
            out_specs=jax.tree.map(lambda _: VMEM, out_shape),
            compiler_params=PARAMS,
            cost_estimate=cost(1000000000 if name == 'render_last' else 1000, 1000),
            name=name,
            **more,
        )(*args)

    def edges_of(parts):
        count = chip_depth * len(parts)
        group = LANES // 8
        shapes = (
            jax.ShapeDtypeStruct((2, -(-count // group) * group, 8, LANES), f32),
            jax.ShapeDtypeStruct((sent_tiles(count), 8, LANES), f32),
        )
        kernel = functools.partial(edge_kernel, chip_depth, own)
        edges, sent = pl.pallas_call(
            kernel,
            out_shape=shapes,
            in_specs=[VMEM] * len(parts),
            out_specs=(VMEM, VMEM),
            compiler_params=PARAMS,
            cost_estimate=cost(1000, 1000),
            name="edge_columns",
        )(*parts)
        if columns == 2:
            return (edges,) + (lax.ppermute(sent, "cols", [(0, 1), (1, 0)]),) * 2
        return (edges,) + tuple(
            lax.ppermute(sent, "cols", [(i, i + shift) for i in range(columns) if 0 <= i + shift < columns])
            for shift in (1, -1)
        )

    def render_call(last, parts):
        count = depth * size + (6 if last else 2)
        scratch = [pltpu.VMEM((count, own + 24, width), f32)] + [pltpu.VMEM((count - 3, own + 8, width), f32)] * 3
        kernel = functools.partial(render_kernel, size, chip_depth, last)
        name = "render_last" if last else "render_first"
        return call(kernel, name, image, info, weights, *parts, scratch_shapes=scratch)

    def edge_scratch(last):
        return [pltpu.VMEM((depth * size + (6 if last else 2), 8, 2 * LANES), f32)] * 2

    def swap(x, bits):
        return lax.ppermute(x, "depth", [(i, i ^ bits) for i in range(groups)])

    def gathered(parts):
        return [parts[0]] + [swap(parts[step], 2 * step) for step in range(1, steps)]

    near = pltpu.VMEM((sent_tiles(chip_depth * steps), 8, LANES), f32)
    _, before, after = edges_of(blocks[steps:])
    ours = call(
        functools.partial(near_kernel, chip_depth),
        "lay_columns",
        (wide_block,) * steps,
        info,
        before,
        after,
        *blocks[steps:],
        scratch_shapes=[near],
        input_output_aliases={3 + i: i for i in range(steps)},
    )
    theirs = gathered(blocks[:steps])
    loose = theirs
    theirs, _ = lax.optimization_barrier((theirs, ours))
    boundary = swap(call(functools.partial(pick_kernel, size), "pick_boundary", block, info, *theirs), size)
    drawn = render_call(False, theirs)
    first_image = call(
        functools.partial(fix_kernel, size, chip_depth),
        "first_edges",
        jax.ShapeDtypeStruct((4 * own + near_rows, width), f32),
        info,
        drawn,
        *edges_of(theirs),
        scratch_shapes=edge_scratch(False) + [near],
    )
    image_part = swap(first_image, size)
    mine = [ours[0]]
    for step in range(1, steps):
        held, _ = lax.optimization_barrier((ours[step], loose[step]))
        mine.append(swap(held, 2 * step))
    parts, _ = lax.optimization_barrier((mine + [boundary], first_image))
    own_part = render_call(True, parts)
    planes = jax.ShapeDtypeStruct((depth * size + 6, 8, 2 * LANES), f32)
    mine_edges = [pltpu.VMEM((2, -(-chip_depth * steps // (LANES // 8)) * (LANES // 8), 8, LANES), f32)]
    kernel = functools.partial(own_edges_kernel, size, chip_depth, own)
    filtered = call(kernel, "own_edges", (planes, planes), info, *parts[:-1], scratch_shapes=mine_edges)
    return call(
        functools.partial(join_kernel, size, chip_depth),
        "join_halves",
        (image, planes, planes),
        info,
        own_part,
        image_part,
        parts[-1],
        *filtered,
        scratch_shapes=[pltpu.VMEM((2, LANES // 8, 8, LANES), f32)],
        input_output_aliases={4: 1, 5: 2},
    )[0]


def solution(mesh):
    return jax.shard_map(
        local,
        mesh=mesh,
        in_specs=(P("depth", None, "cols"),),
        out_specs=P(None, "depth", "cols"),
        check_vma=False,
    )
```

```python
import functools
import math

import jax
import jax.numpy as jnp
import numpy as np
from jax import lax
from jax.experimental import pallas as pl
from jax.experimental.pallas import tpu as pltpu
from jax.sharding import PartitionSpec as P

GAUSS = (1.0, 4.0, 6.0, 4.0, 1.0)
DERIV = (-1.0, -2.0, 0.0, 2.0, 1.0)
SCALE = 7.0 / 4096.0
ONE = 49.0 / 256.0
HALF_LEN = math.sqrt(0.48 * 0.48 + 0.6 * 0.6 + 1.64 * 1.64)
SPEC = 0.35 / HALF_LEN**8
LANES = 128
TILE = 32


def column_weights(width):
    body = np.zeros((width, 2 * width), np.float32)
    for out in range(width):
        for k in range(5):
            if 0 <= out - 2 + k < width:
                body[out - 2 + k, out] = SCALE * GAUSS[k]
                body[out - 2 + k, width + out] = SCALE * DERIV[k]
    return np.concatenate([body, body, body], 0).astype(jnp.bfloat16)


def three_parts(x):
    hi = x.astype(jnp.bfloat16)
    rest = x - hi.astype(jnp.float32)
    mid = rest.astype(jnp.bfloat16)
    lo = (rest - mid.astype(jnp.float32)).astype(jnp.bfloat16)
    return hi, mid, lo


def filter_columns(planes, first, count, weights, sx, dx):
    rows, width = planes.shape[1:]
    flat = planes[first : first + count].reshape(count * rows, width)
    both = jnp.dot(jnp.concatenate(three_parts(flat), 1), weights[...], preferred_element_type=jnp.float32)
    sx[first : first + count] = both[:, :width].reshape(count, rows, width)
    dx[first : first + count] = both[:, width:].reshape(count, rows, width)


def gauss_rows(a, b, c, d, e):
    return (a + e) + 4.0 * (b + d) + 6.0 * c


def shade(t, gx, gy, gz, state):
    v_sum, vt_sum, vu_sum, cover = state
    opacity = pl.reciprocal(1.0 / 0.6 + jnp.exp(jnp.minimum((13.2 - math.log(0.6)) - 6.0 * t, 80.0)))
    tanh_t = jnp.tanh(t)
    tanh_u = jnp.tanh(t + 0.25)
    light = 0.48 * gx + 0.6 * gy + 0.64 * gz
    inv = lax.rsqrt(gx * gx + gy * gy + gz * gz + ONE)
    diffuse = jnp.maximum(light, 0.0) * inv
    half = jnp.maximum(light + gz, 0.0) * inv
    half = half * half
    half = half * half
    shading = 0.25 + 0.6 * diffuse + SPEC * (half * half)
    part = (1.0 - cover) * opacity
    value = part * shading
    return v_sum + value, vt_sum + value * tanh_t, vu_sum + value * tanh_u, cover + part


def render(smooth_rows, slope_rows, shape, count):
    zero = jnp.zeros(shape, jnp.float32)
    state = (zero, zero, zero, zero)
    chains = [[None] * 4 for _ in range(3)]
    for index in range(count + 4):
        a, b, c, d, e = smooth_rows(index)
        inputs = [gauss_rows(a, b, c, d, e), (e - a) + 2.0 * (d - b), gauss_rows(*slope_rows(index))]
        totals, diff = [], None
        for which, (chain, x) in enumerate(zip(chains, inputs)):
            for level in range(4):
                before, chain[level] = chain[level], x
                if before is None:
                    x = None
                    break
                if which == 0 and level == 3:
                    diff = x - before
                x = x + before
            totals.append(x)
        if index >= 4:
            state = shade(totals[0], totals[2], totals[1], diff, state)
    return state


def over(front, back):
    rest = 1.0 - front[3]
    return tuple(f + rest * b for f, b in zip(front, back))


def plane_slots(size, depth, last, info):
    planes = depth * (size // 2)
    extra = 4 if last else 0
    chip, front = info[0], info[2]
    start = 2 * front + extra * (1 - front)
    slots = [(chip ^ step) * depth + plane + start for step in range(size // 2) for plane in range(depth)]
    return slots + [(planes + 2) * front + plane for plane in range(extra)], (1 - front) * (planes + extra)


def render_kernel(size, depth, last, info, weights, *refs):
    blocks, (image, planes, cubed, sx, dx) = refs[:-5], refs[-5:]
    own, width = image.shape[1:]
    slots, empty = plane_slots(size, depth, last, info)
    planes[pl.ds(empty, 2)] = jnp.zeros((2,) + planes.shape[1:], jnp.float32)
    places = [(block, plane) for block in blocks for plane in range(depth)]
    for (block, plane), slot in zip(places, slots):
        around = depth * own + 4 * plane
        planes[slot, 8 : 8 + own] = block[plane * own : (plane + 1) * own]
        planes[slot, 6:8] = block[around : around + 2]
        planes[slot, 8 + own : 10 + own] = block[around + 2 : around + 4]

    def cube(first, rows):
        chain = [None] * 3
        for index in range(planes.shape[0]):
            a, b, c, d = (planes[index, pl.ds(first + 6 + k, rows), :] for k in range(4))
            x = (a + d) + 3.0 * (b + c)
            for level in range(3):
                before, chain[level] = chain[level], x
                if before is None:
                    x = None
                    break
                x = x + before
            if x is not None:
                cubed[index - 3, pl.ds(first, rows), :] = x

    @pl.loop(0, own // TILE)
    def _(tile):
        cube(pl.multiple_of(tile * TILE, TILE), TILE)

    cube(own, 8)
    group = 8
    for index in range(0, cubed.shape[0], group):
        filter_columns(cubed, index, min(group, cubed.shape[0] - index), weights, sx, dx)

    @pl.loop(0, own // TILE)
    def _(tile):
        first = pl.multiple_of(tile * TILE, TILE)
        zero = jnp.zeros((TILE, width), jnp.float32)
        state = (zero, zero, zero, zero)
        for index in range(cubed.shape[0]):
            a, b, c, d = (ref[index, pl.ds(first + k, TILE), :] for ref in (sx, dx) for k in range(2))
            now = (a + b, b - a, c + d)
            if index:
                t, gy, gx = (x + y for x, y in zip(before, now))
                state = shade(t, gx, gy, now[0] - before[0], state)
            before = now
        for channel in range(4):
            image[channel, pl.ds(first, TILE), :] = state[channel]


def edge_columns(blocks, depth, own, out):
    width = blocks[0].shape[1]
    places = [(block, plane) for block in blocks for plane in range(depth)]
    group = LANES // 8
    for base in range(0, len(places), group):
        for part, count in enumerate((own, 4)):
            lane = lax.broadcasted_iota(jnp.int32, (count, width), 1) // 8
            packed = jnp.zeros((count, width), jnp.float32)
            for at, (block, plane) in enumerate(places[base : base + group]):
                first = part * depth * own + plane * count
                turned = pltpu.roll(block[first : first + count], (8 * at + 4) % width, 1)
                packed = jnp.where(lane == at, turned, packed)
            if count < LANES:
                packed = jnp.concatenate([packed, jnp.zeros((LANES - count, width), jnp.float32)], 0)
            out[part, base : base + group] = jnp.transpose(packed).reshape(group, 8, LANES)


def sent_tiles(count):
    return -(-count // 2) + -(-count // (LANES // 4))


def edge_kernel(depth, own, *refs):
    blocks, (out, sent) = refs[:-2], refs[-2:]
    edge_columns(blocks, depth, own, out)
    count = depth * len(blocks)
    line = lax.broadcasted_iota(jnp.int32, (8, LANES), 0)
    pairs = -(-count // 2)
    for pair in range(pairs):
        sent[pair] = jnp.where(line < 4, pltpu.roll(out[0, 2 * pair], 6, 0), pltpu.roll(out[0, 2 * pair + 1], 2, 0))
    lane = lax.broadcasted_iota(jnp.int32, (8, LANES), 1) // 4
    for base in range(0, count, LANES // 4):
        packed = jnp.zeros((8, LANES), jnp.float32)
        for at in range(min(LANES // 4, count - base)):
            packed = jnp.where(lane == at, pltpu.roll(out[1, base + at], 4 * at, 1), packed)
        sent[pairs + base // (LANES // 4)] = packed


def near_tiles(info, count, before, after, near):
    pairs = -(-count // 2)
    left = jnp.where(info[3] == 1, before[...], 0.0)
    right = jnp.where(info[4] == 1, after[...], 0.0)
    line = lax.broadcasted_iota(jnp.int32, left.shape, 1)
    near[0:pairs] = jnp.where(line % 4 < 2, left, right)[0:pairs]
    near[pairs:] = jnp.where(line < 4, left, right)[pairs:]


def block_near(near, depth, blocks, block):
    pairs, group = depth // 2, LANES // (4 * depth)
    turn = LANES - block % group * (4 * depth)
    around = pltpu.roll(near[blocks * pairs + block // group], turn % LANES, 1)
    return [near[block * pairs + pair] for pair in range(pairs)] + [around]


def near_kernel(depth, info, before, after, *refs):
    blocks, near = refs[(len(refs) - 1) // 2 : -1], refs[-1]
    near_tiles(info, depth * len(blocks), before, after, near)
    for index, out in enumerate(blocks):
        tiles = block_near(near, depth, len(blocks), index)
        first = out.shape[0] - 8 * len(tiles)
        for at, tile in enumerate(tiles):
            out[first + 8 * at : first + 8 * at + 8] = tile


def neighbour_columns(depth, tiles):
    own, around = [], []
    for block in tiles:
        for plane in range(depth):
            own.append(pltpu.roll(block[plane // 2], 6 if plane % 2 else 2, 0))
            around.append(pltpu.roll(block[-1], (LANES - 4 * plane) % LANES, 1))
    return jnp.stack(own, 0), jnp.stack(around, 0)


def filter_edges(own, mine, tiles, depth, slots, sx, dx):
    count = len(slots)
    lane = lax.broadcasted_iota(jnp.int32, (count, 8, LANES), 2)
    line = lax.broadcasted_iota(jnp.int32, (count, 8, 2 * LANES), 1)

    def all_rows(main, around):
        if own < LANES:
            main = jnp.where(lane < own, main, pltpu.roll(around, own - 2, 2))
        return jnp.concatenate([main, pltpu.roll(around, LANES - 2, 2)], 2)

    mid = all_rows(mine[0, 0:count], mine[1, 0:count])
    beside = all_rows(*neighbour_columns(depth, tiles))
    end = jnp.where(line < 4, mid, beside)
    top = jnp.where(line < 4, beside, mid)
    taps = [jnp.where(line < 2, end, top)]
    for k in range(1, 5):
        taps.append(jnp.where(line < 2, pltpu.roll(end, 8 - k, 1), pltpu.roll(top, 8 - k, 1)))
    a, b, c, d, e = taps
    smooth = SCALE * gauss_rows(a, b, c, d, e)
    slope = SCALE * ((e - a) + 2.0 * (d - b))
    for index, slot in enumerate(slots):
        sx[slot] = smooth[index]
        dx[slot] = slope[index]


def clear_planes(empty, *planes):
    for out in planes:
        out[pl.ds(empty, 2)] = jnp.zeros((2,) + out.shape[1:], jnp.float32)


def render_edges(sx, dx):
    def rows_of(ref):
        def five(index):
            rows = ref[index]
            return [pltpu.roll(rows, k % (2 * LANES), 1)[:, :LANES] for k in (2, 1, 0, -1, -2)]

        return five

    return render(rows_of(sx), rows_of(dx), (8, LANES), sx.shape[0] - 4)


def with_edges(state, image):
    own, width = image.shape[1:]
    rows = jnp.concatenate(list(state) + [jnp.zeros((LANES - 32, LANES), jnp.float32)], 0)
    columns = jnp.transpose(rows)[0:own]
    lane = lax.broadcasted_iota(jnp.int32, columns.shape, 1)
    inside = (lane >= 2) & (lane < width - 2)
    return [
        jnp.where(inside, image[channel], pltpu.roll(columns, width - 2 - 8 * channel, 1)) for channel in range(4)
    ]


def fix_kernel(size, depth, info, image, mine, before, after, out, sx, dx, near):
    steps, own = size // 2, image.shape[1]
    near_tiles(info, depth * steps, before, after, near)
    tiles = [block_near(near, depth, steps, step) for step in range(steps)]
    slots, empty = plane_slots(size, depth, False, info)
    clear_planes(empty, sx, dx)
    filter_edges(own, mine, tiles, depth, slots, sx, dx)
    state = render_edges(sx, dx)
    for channel, values in enumerate(with_edges(state, image)):
        out[channel * own : (channel + 1) * own] = values
    wanted = info[0] ^ (info[2] * (steps - 1))
    for step in range(steps):

        @pl.when(wanted == step)
        def _():
            for at, tile in enumerate(tiles[step]):
                out[4 * own + 8 * at : 4 * own + 8 * at + 8] = tile


def block_tiles(source, depth):
    first = source.shape[0] - 8 * (depth // 2 + 1)
    return [source[first + 8 * at : first + 8 * at + 8] for at in range(depth // 2 + 1)]


def own_edges_kernel(size, depth, own, info, *refs):
    blocks, (sx, dx, mine) = refs[:-3], refs[-3:]
    edge_columns(blocks, depth, own, mine)
    slots, empty = plane_slots(size, depth, True, info)
    clear_planes(empty, sx, dx)
    tiles = [block_tiles(block, depth) for block in blocks]
    filter_edges(own, mine, tiles, depth, slots[:-4], sx, dx)


def join_kernel(size, depth, info, image, other, boundary, sx_own, dx_own, picture, sx, dx, mine):
    own = image.shape[1]
    edge_columns([boundary], depth, own, mine)
    filter_edges(own, mine, [block_tiles(other, depth)], depth, plane_slots(size, depth, True, info)[0][-4:], sx, dx)
    mine = with_edges(render_edges(sx, dx), image)
    is_front = info[2] == 1
    other = tuple(other[channel * own : (channel + 1) * own] for channel in range(4))
    ahead = tuple(jnp.where(is_front, m, o) for m, o in zip(mine, other))
    behind = tuple(jnp.where(is_front, o, m) for m, o in zip(mine, other))
    v_sum, vt_sum, vu_sum, cover = over(ahead, behind)
    picture[0] = 0.5 * (v_sum + vu_sum)
    picture[1] = 0.5 * v_sum + 0.4 * vt_sum
    picture[2] = 0.5 * (v_sum - vt_sum)
    picture[3] = cover


def rows_around(field, plane, target, own):
    height, width = field.shape[1:]
    line = lax.broadcasted_iota(jnp.int32, (8, width), 0)
    start = target * own
    above = pl.multiple_of(jnp.maximum(start - 8, 0), 8)
    below = pl.multiple_of(jnp.minimum(start + own, height - 8), 8)
    top = jnp.where(target > 0, pltpu.roll(field[plane, pl.ds(above, 8), :], 2, 0), 0.0)
    end = jnp.where(start + own < height, pltpu.roll(field[plane, pl.ds(below, 8), :], 2, 0), 0.0)
    return jnp.where(line < 2, top, jnp.where(line < 4, end, 0.0))


def targets(size, info):
    chip, core, front = info[0], info[1], info[2]
    for chunk in range(2):
        base = front * size if chunk == 0 else (1 - front) * size
        for step in range(size // 2):
            yield chunk * (size // 2) + step, base + 2 * (chip ^ step), core


def pack_kernel(size, own, shared, info, source, *refs):
    outs = refs[-size:]
    depth, width = source.shape[0], source.shape[2]
    line = lax.broadcasted_iota(jnp.int32, (8, width), 0)
    for index, target, core in targets(size, info):
        out, target, place = outs[index], target + core, 1 - core if shared else core
        start = pl.multiple_of(target * own, 8)
        for plane in range(depth):
            to = pl.multiple_of((place * depth + plane) * own, 8)
            out[pl.ds(to, own), :] = source[plane, pl.ds(start, own), :]
        for plane in range(0, depth, 2):
            first, second = (rows_around(source, plane + k, target, own) for k in range(2))
            to = pl.multiple_of(2 * depth * own + 4 * (place * depth + plane), 8)
            out[pl.ds(to, 8), :] = jnp.where(line < 4, first, pltpu.roll(second, 4, 0))
        if not shared:
            used = 2 * depth * (own + 4)
            out[used:] = jnp.zeros((out.shape[0] - used, width), jnp.float32)


def pick_kernel(size, info, *refs):
    blocks, out = refs[:-1], refs[-1]
    wanted = info[0] ^ (info[2] * (size // 2 - 1))
    for step, block in enumerate(blocks):

        @pl.when(wanted == step)
        def _():
            out[...] = block[...]


SMEM = pl.BlockSpec(memory_space=pltpu.SMEM)
VMEM = pl.BlockSpec(memory_space=pltpu.VMEM)
PARAMS = pltpu.CompilerParams(vmem_limit_bytes=20 * 1024 * 1024)


def cost(flops, size):
    return pl.CostEstimate(flops=flops, bytes_accessed=size, transcendentals=0)


def local(field):
    groups = lax.axis_size("depth")
    columns = lax.axis_size("cols")
    size = groups // 2
    depth, height, width = field.shape
    own = height // groups
    me = lax.axis_index("depth")
    column = lax.axis_index("cols")
    has_left, has_right = column > 0, column < columns - 1
    info = jnp.stack([me % size // 2, me % 2, 1 - me // size, has_left, has_right]).astype(jnp.int32)
    weights = jnp.asarray(column_weights(width))
    f32 = jnp.float32
    steps = size // 2
    chip_depth = 2 * depth
    near_rows = 8 * (chip_depth // 2 + 1)
    block = wide_block = jax.ShapeDtypeStruct((chip_depth * (own + 4) + near_rows, width), f32)
    image = jax.ShapeDtypeStruct((4, own, width), f32)

    shared = lax.ppermute(field, "depth", [(i, i ^ 1) for i in range(groups)])
    blocks = ()
    for source in (field, shared):
        blocks = pl.pallas_call(
            functools.partial(pack_kernel, size, own, source is shared),
            out_shape=(block,) * steps + (wide_block,) * steps,
            in_specs=[SMEM, VMEM] + [VMEM] * len(blocks),
            out_specs=(VMEM,) * size,
            input_output_aliases={2 + i: i for i in range(len(blocks))},
            compiler_params=PARAMS,
            name="pack_shared" if source is shared else "pack_own",
        )(info, source, *blocks)

    def call(kernel, name, out_shape, *args, **more):
        return pl.pallas_call(
            kernel,
            out_shape=out_shape,
            in_specs=[SMEM] + [VMEM] * (len(args) - 1),
            out_specs=jax.tree.map(lambda _: VMEM, out_shape),
            compiler_params=PARAMS,
            cost_estimate=cost(1_000_000_000 if name == "render_last" else 1000, 1000),
            name=name,
            **more,
        )(*args)

    def edges_of(parts):
        count = chip_depth * len(parts)
        group = LANES // 8
        shapes = (
            jax.ShapeDtypeStruct((2, -(-count // group) * group, 8, LANES), f32),
            jax.ShapeDtypeStruct((sent_tiles(count), 8, LANES), f32),
        )
        kernel = functools.partial(edge_kernel, chip_depth, own)
        edges, sent = pl.pallas_call(
            kernel,
            out_shape=shapes,
            in_specs=[VMEM] * len(parts),
            out_specs=(VMEM, VMEM),
            compiler_params=PARAMS,
            cost_estimate=cost(1000, 1000),
            name="edge_columns",
        )(*parts)
        if columns == 2:
            return (edges,) + (lax.ppermute(sent, "cols", [(0, 1), (1, 0)]),) * 2
        return (edges,) + tuple(
            lax.ppermute(sent, "cols", [(i, i + shift) for i in range(columns) if 0 <= i + shift < columns])
            for shift in (1, -1)
        )

    def render_call(last, parts):
        count = depth * size + (6 if last else 2)
        scratch = [pltpu.VMEM((count, own + 24, width), f32)] + [pltpu.VMEM((count - 3, own + 8, width), f32)] * 3
        kernel = functools.partial(render_kernel, size, chip_depth, last)
        name = "render_last" if last else "render_first"
        return call(kernel, name, image, info, weights, *parts, scratch_shapes=scratch)

    def edge_scratch(last):
        return [pltpu.VMEM((depth * size + (6 if last else 2), 8, 2 * LANES), f32)] * 2

    def swap(x, bits):
        return lax.ppermute(x, "depth", [(i, i ^ bits) for i in range(groups)])

    def gathered(parts):
        return [parts[0]] + [swap(parts[step], 2 * step) for step in range(1, steps)]

    near = pltpu.VMEM((sent_tiles(chip_depth * steps), 8, LANES), f32)
    _, before, after = edges_of(blocks[steps:])
    ours = call(
        functools.partial(near_kernel, chip_depth),
        "lay_columns",
        (wide_block,) * steps,
        info,
        before,
        after,
        *blocks[steps:],
        scratch_shapes=[near],
        input_output_aliases={3 + i: i for i in range(steps)},
    )
    theirs = gathered(blocks[:steps])
    loose = theirs
    theirs, _ = lax.optimization_barrier((theirs, ours))
    boundary = swap(call(functools.partial(pick_kernel, size), "pick_boundary", block, info, *theirs), size)
    drawn = render_call(False, theirs)
    first_image = call(
        functools.partial(fix_kernel, size, chip_depth),
        "first_edges",
        jax.ShapeDtypeStruct((4 * own + near_rows, width), f32),
        info,
        drawn,
        *edges_of(theirs),
        scratch_shapes=edge_scratch(False) + [near],
    )
    image_part = swap(first_image, size)
    mine = [ours[0]]
    for step in range(1, steps):
        held, _ = lax.optimization_barrier((ours[step], loose[step]))
        mine.append(swap(held, 2 * step))
    parts, _ = lax.optimization_barrier((mine + [boundary], first_image))
    own_part = render_call(True, parts)
    planes = jax.ShapeDtypeStruct((depth * size + 6, 8, 2 * LANES), f32)
    mine_edges = [pltpu.VMEM((2, -(-chip_depth * steps // (LANES // 8)) * (LANES // 8), 8, LANES), f32)]
    kernel = functools.partial(own_edges_kernel, size, chip_depth, own)
    filtered = call(kernel, "own_edges", (planes, planes), info, *parts[:-1], scratch_shapes=mine_edges)
    return call(
        functools.partial(join_kernel, size, chip_depth),
        "join_halves",
        (image, planes, planes),
        info,
        own_part,
        image_part,
        parts[-1],
        *filtered,
        scratch_shapes=[pltpu.VMEM((2, LANES // 8, 8, LANES), f32)],
        input_output_aliases={4: 1, 5: 2},
    )[0]


def solution(mesh):
    return jax.shard_map(
        local,
        mesh=mesh,
        in_specs=(P("depth", None, "cols"),),
        out_specs=P(None, "depth", "cols"),
        check_vma=False,
    )
```

```python
import functools
import math

import jax
import jax.numpy as jnp
import numpy as np
from jax import lax
from jax.experimental import pallas as pl
from jax.experimental.pallas import tpu as pltpu
from jax.sharding import PartitionSpec as P

GAUSS = (1.0, 4.0, 6.0, 4.0, 1.0)
DERIV = (-1.0, -2.0, 0.0, 2.0, 1.0)
SCALE = 7.0 / 4096.0
ONE = 49.0 / 256.0
HALF_LEN = math.sqrt(0.48 * 0.48 + 0.6 * 0.6 + 1.64 * 1.64)
SPEC = 0.35 / HALF_LEN**8
LANES = 128
TILE = 32


def column_weights(width):
    body = np.zeros((width, 2 * width), np.float32)
    for out in range(width):
        for k in range(5):
            if 0 <= out - 2 + k < width:
                body[out - 2 + k, out] = SCALE * GAUSS[k]
                body[out - 2 + k, width + out] = SCALE * DERIV[k]
    return np.concatenate([body, body, body], 0).astype(jnp.bfloat16)


def three_parts(x):
    hi = x.astype(jnp.bfloat16)
    rest = x - hi.astype(jnp.float32)
    mid = rest.astype(jnp.bfloat16)
    lo = (rest - mid.astype(jnp.float32)).astype(jnp.bfloat16)
    return hi, mid, lo


def filter_columns(planes, first, count, weights, sx, dx):
    rows, width = planes.shape[1:]
    flat = planes[first : first + count].reshape(count * rows, width)
    both = jnp.dot(jnp.concatenate(three_parts(flat), 1), weights[...], preferred_element_type=jnp.float32)
    sx[first : first + count] = both[:, :width].reshape(count, rows, width)
    dx[first : first + count] = both[:, width:].reshape(count, rows, width)


def gauss_rows(a, b, c, d, e):
    return (a + e) + 4.0 * (b + d) + 6.0 * c


def shade(t, gx, gy, gz, state):
    v_sum, vt_sum, vu_sum, cover = state
    opacity = pl.reciprocal(1.0 / 0.6 + jnp.exp(jnp.minimum((13.2 - math.log(0.6)) - 6.0 * t, 80.0)))
    tanh_t = jnp.tanh(t)
    tanh_u = jnp.tanh(t + 0.25)
    light = 0.48 * gx + 0.6 * gy + 0.64 * gz
    inv = lax.rsqrt(gx * gx + gy * gy + gz * gz + ONE)
    diffuse = jnp.maximum(light, 0.0) * inv
    half = jnp.maximum(light + gz, 0.0) * inv
    half = half * half
    half = half * half
    shading = 0.25 + 0.6 * diffuse + SPEC * (half * half)
    part = (1.0 - cover) * opacity
    value = part * shading
    return v_sum + value, vt_sum + value * tanh_t, vu_sum + value * tanh_u, cover + part


def render(smooth_rows, slope_rows, shape, count):
    zero = jnp.zeros(shape, jnp.float32)
    state = (zero, zero, zero, zero)
    chains = [[None] * 4 for _ in range(3)]
    for index in range(count + 4):
        a, b, c, d, e = smooth_rows(index)
        inputs = [gauss_rows(a, b, c, d, e), (e - a) + 2.0 * (d - b), gauss_rows(*slope_rows(index))]
        totals, diff = [], None
        for which, (chain, x) in enumerate(zip(chains, inputs)):
            for level in range(4):
                before, chain[level] = chain[level], x
                if before is None:
                    x = None
                    break
                if which == 0 and level == 3:
                    diff = x - before
                x = x + before
            totals.append(x)
        if index >= 4:
            state = shade(totals[0], totals[2], totals[1], diff, state)
    return state


def over(front, back):
    rest = 1.0 - front[3]
    return tuple(f + rest * b for f, b in zip(front, back))


def plane_slots(size, depth, last, info):
    planes = depth * (size // 2)
    extra = 4 if last else 0
    chip, front = info[0], info[2]
    start = 2 * front + extra * (1 - front)
    slots = [(chip ^ step) * depth + plane + start for step in range(size // 2) for plane in range(depth)]
    return slots + [(planes + 2) * front + plane for plane in range(extra)], (1 - front) * (planes + extra)


def render_kernel(size, depth, last, info, weights, *refs):
    blocks, (image, planes, cubed, sx, dx) = refs[:-5], refs[-5:]
    own, width = image.shape[1:]
    slots, empty = plane_slots(size, depth, last, info)
    planes[pl.ds(empty, 2)] = jnp.zeros((2,) + planes.shape[1:], jnp.float32)
    places = [(block, plane) for block in blocks for plane in range(depth)]
    for (block, plane), slot in zip(places, slots):
        around = depth * own + 4 * plane
        planes[slot, 8 : 8 + own] = block[plane * own : (plane + 1) * own]
        planes[slot, 6:8] = block[around : around + 2]
        planes[slot, 8 + own : 10 + own] = block[around + 2 : around + 4]

    def cube(first, rows):
        chain = [None] * 3
        for index in range(planes.shape[0]):
            a, b, c, d = (planes[index, pl.ds(first + 6 + k, rows), :] for k in range(4))
            x = (a + d) + 3.0 * (b + c)
            for level in range(3):
                before, chain[level] = chain[level], x
                if before is None:
                    x = None
                    break
                x = x + before
            if x is not None:
                cubed[index - 3, pl.ds(first, rows), :] = x

    @pl.loop(0, own // TILE)
    def _(tile):
        cube(pl.multiple_of(tile * TILE, TILE), TILE)

    cube(own, 8)
    group = 8
    for index in range(0, cubed.shape[0], group):
        filter_columns(cubed, index, min(group, cubed.shape[0] - index), weights, sx, dx)

    @pl.loop(0, own // TILE)
    def _(tile):
        first = pl.multiple_of(tile * TILE, TILE)
        zero = jnp.zeros((TILE, width), jnp.float32)
        state = (zero, zero, zero, zero)
        for index in range(cubed.shape[0]):
            a, b, c, d = (ref[index, pl.ds(first + k, TILE), :] for ref in (sx, dx) for k in range(2))
            now = (a + b, b - a, c + d)
            if index:
                t, gy, gx = (x + y for x, y in zip(before, now))
                state = shade(t, gx, gy, now[0] - before[0], state)
            before = now
        for channel in range(4):
            image[channel, pl.ds(first, TILE), :] = state[channel]


def edge_columns(blocks, depth, own, out):
    width = blocks[0].shape[1]
    places = [(block, plane) for block in blocks for plane in range(depth)]
    group = LANES // 8
    for base in range(0, len(places), group):
        for part, count in enumerate((own, 4)):
            lane = lax.broadcasted_iota(jnp.int32, (count, width), 1) // 8
            packed = jnp.zeros((count, width), jnp.float32)
            for at, (block, plane) in enumerate(places[base : base + group]):
                first = part * depth * own + plane * count
                turned = pltpu.roll(block[first : first + count], (8 * at + 4) % width, 1)
                packed = jnp.where(lane == at, turned, packed)
            if count < LANES:
                packed = jnp.concatenate([packed, jnp.zeros((LANES - count, width), jnp.float32)], 0)
            out[part, base : base + group] = jnp.transpose(packed).reshape(group, 8, LANES)


def sent_tiles(count):
    return -(-count // 2) + -(-count // (LANES // 4))


def edge_kernel(depth, own, *refs):
    blocks, (out, sent) = refs[:-2], refs[-2:]
    edge_columns(blocks, depth, own, out)
    count = depth * len(blocks)
    line = lax.broadcasted_iota(jnp.int32, (8, LANES), 0)
    pairs = -(-count // 2)
    for pair in range(pairs):
        sent[pair] = jnp.where(line < 4, pltpu.roll(out[0, 2 * pair], 6, 0), pltpu.roll(out[0, 2 * pair + 1], 2, 0))
    lane = lax.broadcasted_iota(jnp.int32, (8, LANES), 1) // 4
    for base in range(0, count, LANES // 4):
        packed = jnp.zeros((8, LANES), jnp.float32)
        for at in range(min(LANES // 4, count - base)):
            packed = jnp.where(lane == at, pltpu.roll(out[1, base + at], 4 * at, 1), packed)
        sent[pairs + base // (LANES // 4)] = packed


def near_tiles(info, count, before, after, near):
    pairs = -(-count // 2)
    left = jnp.where(info[3] == 1, before[...], 0.0)
    right = jnp.where(info[4] == 1, after[...], 0.0)
    line = lax.broadcasted_iota(jnp.int32, left.shape, 1)
    near[0:pairs] = jnp.where(line % 4 < 2, left, right)[0:pairs]
    near[pairs:] = jnp.where(line < 4, left, right)[pairs:]


def block_near(near, depth, blocks, block):
    pairs, group = depth // 2, LANES // (4 * depth)
    turn = LANES - block % group * (4 * depth)
    around = pltpu.roll(near[blocks * pairs + block // group], turn % LANES, 1)
    return [near[block * pairs + pair] for pair in range(pairs)] + [around]


def near_kernel(depth, info, before, after, *refs):
    blocks, near = refs[(len(refs) - 1) // 2 : -1], refs[-1]
    near_tiles(info, depth * len(blocks), before, after, near)
    for index, out in enumerate(blocks):
        tiles = block_near(near, depth, len(blocks), index)
        first = out.shape[0] - 8 * len(tiles)
        for at, tile in enumerate(tiles):
            out[first + 8 * at : first + 8 * at + 8] = tile


def neighbour_columns(depth, tiles):
    own, around = [], []
    for block in tiles:
        for plane in range(depth):
            own.append(pltpu.roll(block[plane // 2], 6 if plane % 2 else 2, 0))
            around.append(pltpu.roll(block[-1], (LANES - 4 * plane) % LANES, 1))
    return jnp.stack(own, 0), jnp.stack(around, 0)


def filter_edges(own, mine, tiles, depth, slots, sx, dx):
    count = len(slots)
    lane = lax.broadcasted_iota(jnp.int32, (count, 8, LANES), 2)
    line = lax.broadcasted_iota(jnp.int32, (count, 8, 2 * LANES), 1)

    def all_rows(main, around):
        if own < LANES:
            main = jnp.where(lane < own, main, pltpu.roll(around, own - 2, 2))
        return jnp.concatenate([main, pltpu.roll(around, LANES - 2, 2)], 2)

    mid = all_rows(mine[0, 0:count], mine[1, 0:count])
    beside = all_rows(*neighbour_columns(depth, tiles))
    end = jnp.where(line < 4, mid, beside)
    top = jnp.where(line < 4, beside, mid)
    taps = [jnp.where(line < 2, end, top)]
    for k in range(1, 5):
        taps.append(jnp.where(line < 2, pltpu.roll(end, 8 - k, 1), pltpu.roll(top, 8 - k, 1)))
    a, b, c, d, e = taps
    smooth = SCALE * gauss_rows(a, b, c, d, e)
    slope = SCALE * ((e - a) + 2.0 * (d - b))
    for index, slot in enumerate(slots):
        sx[slot] = smooth[index]
        dx[slot] = slope[index]


def clear_planes(empty, *planes):
    for out in planes:
        out[pl.ds(empty, 2)] = jnp.zeros((2,) + out.shape[1:], jnp.float32)


def render_edges(sx, dx):
    def rows_of(ref):
        def five(index):
            rows = ref[index]
            return [pltpu.roll(rows, k % (2 * LANES), 1)[:, :LANES] for k in (2, 1, 0, -1, -2)]

        return five

    return render(rows_of(sx), rows_of(dx), (8, LANES), sx.shape[0] - 4)


def with_edges(state, image):
    own, width = image.shape[1:]
    rows = jnp.concatenate(list(state) + [jnp.zeros((LANES - 32, LANES), jnp.float32)], 0)
    columns = jnp.transpose(rows)[0:own]
    lane = lax.broadcasted_iota(jnp.int32, columns.shape, 1)
    inside = (lane >= 2) & (lane < width - 2)
    return [
        jnp.where(inside, image[channel], pltpu.roll(columns, width - 2 - 8 * channel, 1)) for channel in range(4)
    ]


def fix_kernel(size, depth, info, image, mine, before, after, out, sx, dx, near):
    steps, own = size // 2, image.shape[1]
    near_tiles(info, depth * steps, before, after, near)
    tiles = [block_near(near, depth, steps, step) for step in range(steps)]
    slots, empty = plane_slots(size, depth, False, info)
    clear_planes(empty, sx, dx)
    filter_edges(own, mine, tiles, depth, slots, sx, dx)
    state = render_edges(sx, dx)
    for channel, values in enumerate(with_edges(state, image)):
        out[channel * own : (channel + 1) * own] = values
    wanted = info[0] ^ (info[2] * (steps - 1))
    for step in range(steps):

        @pl.when(wanted == step)
        def _():
            for at, tile in enumerate(tiles[step]):
                out[4 * own + 8 * at : 4 * own + 8 * at + 8] = tile


def block_tiles(source, depth):
    first = source.shape[0] - 8 * (depth // 2 + 1)
    return [source[first + 8 * at : first + 8 * at + 8] for at in range(depth // 2 + 1)]


def own_edges_kernel(size, depth, own, info, *refs):
    blocks, (sx, dx, mine) = refs[:-3], refs[-3:]
    edge_columns(blocks, depth, own, mine)
    slots, empty = plane_slots(size, depth, True, info)
    clear_planes(empty, sx, dx)
    tiles = [block_tiles(block, depth) for block in blocks]
    filter_edges(own, mine, tiles, depth, slots[:-4], sx, dx)


def join_kernel(size, depth, info, image, other, boundary, sx_own, dx_own, picture, sx, dx, mine, drawn, sems):
    own = image.shape[1]
    edge_columns([boundary], depth, own, mine)
    filter_edges(own, mine, [block_tiles(other, depth)], depth, plane_slots(size, depth, True, info)[0][-4:], sx, dx)
    mine = with_edges(render_edges(sx, dx), image)
    is_front = info[2] == 1
    other = tuple(other[channel * own : (channel + 1) * own] for channel in range(4))
    ahead = tuple(jnp.where(is_front, m, o) for m, o in zip(mine, other))
    behind = tuple(jnp.where(is_front, o, m) for m, o in zip(mine, other))
    v_sum, vt_sum, vu_sum, cover = over(ahead, behind)
    colours = (0.5 * (v_sum + vu_sum), 0.5 * v_sum + 0.4 * vt_sum, 0.5 * (v_sum - vt_sum), cover)
    copies = []
    for channel, values in enumerate(colours):
        drawn[channel] = values
        copies.append(pltpu.make_async_copy(drawn.at[channel], picture.at[channel], sems.at[channel]))
        copies[-1].start()
    for copy in copies:
        copy.wait()


def rows_around(field, plane, target, own):
    height, width = field.shape[1:]
    line = lax.broadcasted_iota(jnp.int32, (8, width), 0)
    start = target * own
    above = pl.multiple_of(jnp.maximum(start - 8, 0), 8)
    below = pl.multiple_of(jnp.minimum(start + own, height - 8), 8)
    top = jnp.where(target > 0, pltpu.roll(field[plane, pl.ds(above, 8), :], 2, 0), 0.0)
    end = jnp.where(start + own < height, pltpu.roll(field[plane, pl.ds(below, 8), :], 2, 0), 0.0)
    return jnp.where(line < 2, top, jnp.where(line < 4, end, 0.0))


def targets(size, info):
    chip, core, front = info[0], info[1], info[2]
    for chunk in range(2):
        base = front * size if chunk == 0 else (1 - front) * size
        for step in range(size // 2):
            yield chunk * (size // 2) + step, base + 2 * (chip ^ step), core


def pack_kernel(size, own, shared, info, source, *refs):
    outs = refs[-size:]
    depth, width = source.shape[0], source.shape[2]
    line = lax.broadcasted_iota(jnp.int32, (8, width), 0)
    for index, target, core in targets(size, info):
        out, target, place = outs[index], target + core, 1 - core if shared else core
        start = pl.multiple_of(target * own, 8)
        for plane in range(depth):
            to = pl.multiple_of((place * depth + plane) * own, 8)
            out[pl.ds(to, own), :] = source[plane, pl.ds(start, own), :]
        for plane in range(0, depth, 2):
            first, second = (rows_around(source, plane + k, target, own) for k in range(2))
            to = pl.multiple_of(2 * depth * own + 4 * (place * depth + plane), 8)
            out[pl.ds(to, 8), :] = jnp.where(line < 4, first, pltpu.roll(second, 4, 0))
        if not shared:
            used = 2 * depth * (own + 4)
            out[used:] = jnp.zeros((out.shape[0] - used, width), jnp.float32)


def pick_kernel(size, info, *refs):
    blocks, out = refs[:-1], refs[-1]
    wanted = info[0] ^ (info[2] * (size // 2 - 1))
    for step, block in enumerate(blocks):

        @pl.when(wanted == step)
        def _():
            out[...] = block[...]


SMEM = pl.BlockSpec(memory_space=pltpu.SMEM)
VMEM = pl.BlockSpec(memory_space=pltpu.VMEM)
PARAMS = pltpu.CompilerParams(vmem_limit_bytes=20 * 1024 * 1024)


def cost(flops, size):
    return pl.CostEstimate(flops=flops, bytes_accessed=size, transcendentals=0)


def local(field):
    groups = lax.axis_size("depth")
    columns = lax.axis_size("cols")
    size = groups // 2
    depth, height, width = field.shape
    own = height // groups
    me = lax.axis_index("depth")
    column = lax.axis_index("cols")
    has_left, has_right = column > 0, column < columns - 1
    info = jnp.stack([me % size // 2, me % 2, 1 - me // size, has_left, has_right]).astype(jnp.int32)
    weights = jnp.asarray(column_weights(width))
    f32 = jnp.float32
    steps = size // 2
    chip_depth = 2 * depth
    near_rows = 8 * (chip_depth // 2 + 1)
    block = wide_block = jax.ShapeDtypeStruct((chip_depth * (own + 4) + near_rows, width), f32)
    image = jax.ShapeDtypeStruct((4, own, width), f32)

    shared = lax.ppermute(field, "depth", [(i, i ^ 1) for i in range(groups)])
    blocks = ()
    for source in (field, shared):
        blocks = pl.pallas_call(
            functools.partial(pack_kernel, size, own, source is shared),
            out_shape=(block,) * steps + (wide_block,) * steps,
            in_specs=[SMEM, VMEM] + [VMEM] * len(blocks),
            out_specs=(VMEM,) * size,
            input_output_aliases={2 + i: i for i in range(len(blocks))},
            compiler_params=PARAMS,
            name="pack_shared" if source is shared else "pack_own",
        )(info, source, *blocks)

    def call(kernel, name, out_shape, *args, specs=None, **more):
        return pl.pallas_call(
            kernel,
            out_shape=out_shape,
            in_specs=[SMEM] + [VMEM] * (len(args) - 1),
            out_specs=specs or jax.tree.map(lambda _: VMEM, out_shape),
            compiler_params=PARAMS,
            cost_estimate=cost(1_000_000_000 if name == "render_last" else 1000, 1000),
            name=name,
            **more,
        )(*args)

    def edges_of(parts):
        count = chip_depth * len(parts)
        group = LANES // 8
        shapes = (
            jax.ShapeDtypeStruct((2, -(-count // group) * group, 8, LANES), f32),
            jax.ShapeDtypeStruct((sent_tiles(count), 8, LANES), f32),
        )
        kernel = functools.partial(edge_kernel, chip_depth, own)
        edges, sent = pl.pallas_call(
            kernel,
            out_shape=shapes,
            in_specs=[VMEM] * len(parts),
            out_specs=(VMEM, VMEM),
            compiler_params=PARAMS,
            cost_estimate=cost(1000, 1000),
            name="edge_columns",
        )(*parts)
        if columns == 2:
            return (edges,) + (lax.ppermute(sent, "cols", [(0, 1), (1, 0)]),) * 2
        return (edges,) + tuple(
            lax.ppermute(sent, "cols", [(i, i + shift) for i in range(columns) if 0 <= i + shift < columns])
            for shift in (1, -1)
        )

    def render_call(last, parts):
        count = depth * size + (6 if last else 2)
        scratch = [pltpu.VMEM((count, own + 24, width), f32)] + [pltpu.VMEM((count - 3, own + 8, width), f32)] * 3
        kernel = functools.partial(render_kernel, size, chip_depth, last)
        name = "render_last" if last else "render_first"
        return call(kernel, name, image, info, weights, *parts, scratch_shapes=scratch)

    def edge_scratch(last):
        return [pltpu.VMEM((depth * size + (6 if last else 2), 8, 2 * LANES), f32)] * 2

    def swap(x, bits):
        return lax.ppermute(x, "depth", [(i, i ^ bits) for i in range(groups)])

    def gathered(parts):
        return [parts[0]] + [swap(parts[step], 2 * step) for step in range(1, steps)]

    near = pltpu.VMEM((sent_tiles(chip_depth * steps), 8, LANES), f32)
    _, before, after = edges_of(blocks[steps:])
    ours = call(
        functools.partial(near_kernel, chip_depth),
        "lay_columns",
        (wide_block,) * steps,
        info,
        before,
        after,
        *blocks[steps:],
        scratch_shapes=[near],
        input_output_aliases={3 + i: i for i in range(steps)},
    )
    theirs = gathered(blocks[:steps])
    loose = theirs
    theirs, _ = lax.optimization_barrier((theirs, ours))
    boundary = swap(call(functools.partial(pick_kernel, size), "pick_boundary", block, info, *theirs), size)
    drawn = render_call(False, theirs)
    first_image = call(
        functools.partial(fix_kernel, size, chip_depth),
        "first_edges",
        jax.ShapeDtypeStruct((4 * own + near_rows, width), f32),
        info,
        drawn,
        *edges_of(theirs),
        scratch_shapes=edge_scratch(False) + [near],
    )
    image_part = swap(first_image, size)
    mine = [ours[0]]
    for step in range(1, steps):
        held, _ = lax.optimization_barrier((ours[step], loose[step]))
        mine.append(swap(held, 2 * step))
    parts, _ = lax.optimization_barrier((mine + [boundary], first_image))
    own_part = render_call(True, parts)
    planes = jax.ShapeDtypeStruct((depth * size + 6, 8, 2 * LANES), f32)
    mine_edges = [pltpu.VMEM((2, -(-chip_depth * steps // (LANES // 8)) * (LANES // 8), 8, LANES), f32)]
    kernel = functools.partial(own_edges_kernel, size, chip_depth, own)
    filtered = call(kernel, "own_edges", (planes, planes), info, *parts[:-1], scratch_shapes=mine_edges)
    return call(
        functools.partial(join_kernel, size, chip_depth),
        "join_halves",
        (image, planes, planes),
        info,
        own_part,
        image_part,
        parts[-1],
        *filtered,
        specs=(pl.BlockSpec(memory_space=pl.ANY), VMEM, VMEM),
        scratch_shapes=[
            pltpu.VMEM((2, LANES // 8, 8, LANES), f32),
            pltpu.VMEM(image.shape, f32),
            pltpu.SemaphoreType.DMA((4,)),
        ],
        input_output_aliases={4: 1, 5: 2},
    )[0]


def solution(mesh):
    return jax.shard_map(
        local,
        mesh=mesh,
        in_specs=(P("depth", None, "cols"),),
        out_specs=P(None, "depth", "cols"),
        check_vma=False,
    )
```
